128 devices in a mesh: role: 2 (over core), dev: 64 (over x, y, z).
Axes of the slice: x: 4, y: 4, z: 4, core: 2. Of those that a mesh axis runs over, the one named last changes fastest.
Arguments:
- queries: bfloat16 [512, 64, 576], P(('role', 'dev'))
- latent_cache: bfloat16 [512, 2048, 576], P(('role', 'dev')), may hold values from -6 to 6, as said below
- lengths: int32 [512], P(('role', 'dev')), may hold values from 1 to 2048, 262144 in all
- residual: bfloat16 [512, 7168], P(('role', 'dev')), may hold values from -3 to 3
- w_uv: bfloat16 [64, 512, 128], P('dev'), may hold values from -0.25 to 0.25
- w_out: bfloat16 [8192, 7168], P('dev'), may hold values from -0.0625 to 0.0625
- norm_gain: bfloat16 [7168], replicated, may hold values from 0.5 to 1.5
- expert_ids: int32 [512, 8], P(('role', 'dev')), may hold values from 0 to 15, all different within a row; in each aligned block of 4 rows (0 to 3, 4 to 7, ...) at most 3 rows name the same one
- gate_values: bfloat16 [512, 8], P(('role', 'dev')), may hold values from 0.099609375 to 0.59765625
- w_gate: bfloat16 [128, 7168, 256], P(('role', 'dev')), may hold values from -0.0625 to 0.0625
- w_up: bfloat16 [128, 7168, 256], P(('role', 'dev')), may hold values from -0.0625 to 0.0625
- w_down: bfloat16 [128, 256, 7168], P(('role', 'dev')), may hold values from -0.125 to 0.125
Outputs:
- layer_out: bfloat16 [512, 7168], P(('role', 'dev'))
The draws below stay inside these ranges and needn't reach their ends.
Inputs may be any that keep to these rules, and one draw needn't show every extreme that they name: `expert_ids`: each row names 8 different experts; among the 4 rows of one device no expert is named more than 3 times, a bound that some block reaches. `lengths`: every row has at least one live position, and some row is 2048 long. `latent_cache`: entries of order one.
All inputs are finite; a program needn't handle non-finite values. No bound on the sum of `lengths` on one device may be relied on, other than what follows from the above.
Results may differ from the reference program's by a relative error of at most 0.012.
Values may be sent and summed in bfloat16 or wider, within the bound.
No kernel may reach another device: no remote copies, remote signals or barrier semaphores. Data moves between devices by JAX's collectives and lax.ppermute only.
A program may use at most 128 MiB of HBM per device.

```python
import math
import jax
import jax.numpy as jnp
import numpy as np
from jax import lax

D = 7168
FF = 2048
LAT = 512
ROPE = 64
VHEAD = 128
TOP = 8
HEADS = 64
EXPERTS = 16
ROWS_DEV = 4
MAXLEN = 2048
CAP = 3
ROWS = 512
SPLIT = 8
FF_SLICE = 256
DEVICES = 128


def cache_values(key):
    base = jnp.clip(jax.random.normal(key, (ROWS, MAXLEN, LAT + ROPE), jnp.float32), -6.0, 6.0)
    second = base[:, 1, :]
    return base.at[:, 1, :].set(second)


def draw_latent_cache(key, part):
    values = cache_values(key)
    return values.astype(jnp.bfloat16)


def draw_queries(key, part):
    own_key = jax.random.fold_in(key, 7)
    noise = jnp.clip(jax.random.normal(own_key, (ROWS, HEADS, LAT + ROPE), jnp.float32), -6.0, 6.0)
    values = noise
    return values.astype(jnp.bfloat16)


def shard_levels(stream_key, dims, split, least, largest):
    loudness = 1.0
    for axis_at, blocks in split:
        draws = jax.random.uniform(jax.random.fold_in(jax.random.fold_in(stream_key, 6), axis_at), (blocks,), jnp.float32, least / len(split), largest / len(split))
        loudness = loudness * jnp.repeat(jnp.exp(draws), dims[axis_at] // blocks).reshape((-1,) + (1,) * (len(dims) - 1 - axis_at))
    return loudness


def split_up(count, total, reach, skew):
    weights = [(1 << 20) // math.isqrt(rank ** skew) + 1 for rank in range(2, count + 1)]
    spare, holding = total - reach - (count - 1), [1] * (count - 1)
    while spare > 0:
        free = [i for i in range(count - 1) if holding[i] < reach]
        whole, left = sum([weights[i] for i in free]), spare
        for i in free:
            addition = min(reach - holding[i], max(1, left * weights[i] // whole), spare)
            holding[i] = holding[i] + addition
            spare = spare - addition
    return np.array([reach] + holding)


def ragged_sizes(key, number_of, total, bound, slope):
    if number_of == 2:
        one = jax.random.randint(key, (), max(1, total - bound), min(bound, total - 1) + 1)
        return jnp.stack([one, total - one])
    sizes = jnp.asarray(split_up(number_of, total, bound, slope), jnp.int32)
    couples = (number_of - 1) // 2
    giver, taker = sizes[1:1 + 2 * couples:2], sizes[2:2 + 2 * couples:2]
    margin = jnp.minimum(giver - 1, bound - taker)
    shifted = jax.random.randint(jax.random.fold_in(key, 1), (couples,), 0, 1 << 20) % (margin + 1)
    sizes = sizes.at[1:1 + 2 * couples:2].set(giver - shifted).at[2:2 + 2 * couples:2].set(taker + shifted)
    return sizes[jax.random.permutation(jax.random.fold_in(key, 2), number_of)]


def assign_block(stream_key, own, number, rows, amount, top, limit, slope):
    ranking = jax.random.permutation(stream_key, amount)
    packed, ordinary = load_shares(amount, rows * top, limit, slope, True), load_shares(amount, rows * top, limit, slope, False)
    places = jnp.arange(amount)

    def named(sizes, rotation):
        used = int((sizes > 0).sum())
        fixed = max(1, used // 4)
        moved = fixed + (places - fixed + rotation * (used - fixed)) % max(1, amount - fixed)
        return jnp.zeros((amount,), jnp.int32).at[ranking[jnp.where(places < fixed, places, moved)]].set(jnp.asarray(sizes, jnp.int32))

    sizes = jnp.where(number % 4 == 0, named(packed, number // 4), named(ordinary, number - number // 4 - 1))
    mixed = jax.random.permutation(jax.random.fold_in(own, 3), amount)
    source_of, taker = mixed[0:amount // 2 * 2:2], mixed[1:amount // 2 * 2:2]
    room = jnp.minimum(sizes[source_of] - 1, limit - sizes[taker]) // 2
    room = jnp.where((source_of == ranking[0]) | (taker == ranking[0]) | (sizes[taker] == 0), 0, jnp.maximum(room, 0))
    moved = jax.random.randint(jax.random.fold_in(own, 4), (amount // 2,), 0, 1 << 20) % (room + 1)
    sizes = sizes.at[source_of].add(-moved).at[taker].add(moved)
    members = jnp.searchsorted(jnp.cumsum(sizes), jnp.arange(rows * top), side="right").astype(jnp.int32)
    table = members.reshape(top, rows).T
    table = table[jax.random.permutation(jax.random.fold_in(own, 1), rows)]
    rotation = jax.random.randint(jax.random.fold_in(own, 2), (rows, 1), 0, top)
    return jnp.take_along_axis(table, (jnp.arange(top)[None, :] + rotation) % top, axis=1)


def load_shares(number_of, total, limit, lean, full):
    loads = [(1 << 20) // math.isqrt(standing ** lean) + 1 for standing in range(1, number_of + 1)]
    largest = limit if full else min(limit, max(-(-total // number_of), total * loads[0] // sum(loads)))
    least = 1 if total - largest >= number_of - 1 else 0
    given, rest = [largest] + [least] * (number_of - 1), total - largest - least * (number_of - 1)
    while rest > 0:
        candidates = [i for i in range(1, number_of) if given[i] < largest] or [i for i in range(1, number_of) if given[i] < limit]
        mass, budget = sum([loads[i] for i in candidates]), rest
        for i in candidates:
            more = min(limit - given[i], max(1, budget * loads[i] // mass), rest)
            given[i] = given[i] + more
            rest = rest - more
    return np.array(given)


def bell_draw(key, dims, deviation, bound, cuts=(), held_as=jnp.bfloat16):
    values = deviation * jax.random.normal(key, dims, jnp.float32)
    if cuts:
        values = values * shard_levels(key, dims, cuts, -0.22, 0.18)
    return jnp.clip(values, -bound, bound).astype(held_as)


def setup_inputs(seed: int = 0) -> dict:
    keys = jax.random.split(jax.random.key(seed), 13)
    queries = draw_queries(jax.random.fold_in(keys[12], 71), 0)
    latent_cache = draw_latent_cache(jax.random.fold_in(keys[12], 71), 0)
    lengths = ragged_sizes(keys[2], ROWS, ROWS * MAXLEN // 4, MAXLEN, 2).astype(jnp.int32)
    residual = bell_draw(keys[3], (ROWS, D), 0.5, 3.0, ((0, 128),))
    w_uv = bell_draw(keys[4], (HEADS, LAT, VHEAD), LAT ** -0.5, 0.25, ((0, 64),))
    w_out = bell_draw(keys[5], (HEADS * VHEAD, D), (HEADS * VHEAD) ** -0.5, 0.0625, ((0, 64),))
    norm_gain = jnp.clip(1.0 + 0.1 * jax.random.normal(keys[6], (D,), jnp.float32), 0.5, 1.5).astype(jnp.bfloat16)
    expert_ids_keys = jax.random.split(jax.random.fold_in(keys[7], 1), ROWS // ROWS_DEV)
    expert_ids_turns = jax.random.permutation(jax.random.fold_in(keys[7], 3), ROWS // ROWS_DEV)
    expert_ids = jax.vmap(lambda own, number: assign_block(jax.random.fold_in(keys[7], 2), own, number, ROWS_DEV, EXPERTS, TOP, CAP, 2))(expert_ids_keys, expert_ids_turns).reshape((ROWS, TOP))
    gate_values = jnp.clip(jnp.exp(math.log(0.59765625) - 1.7917595 * jax.random.uniform(keys[8], (ROWS, TOP), jnp.float32) ** shard_levels(keys[8], (ROWS, TOP), ((0, 128),), -0.2, 0.2)), 0.099609375, 0.59765625).astype(jnp.bfloat16)
    w_gate = bell_draw(keys[9], (DEVICES, D, FF_SLICE), D ** -0.5, 0.0625, ((0, 128),))
    w_up = bell_draw(keys[10], (DEVICES, D, FF_SLICE), D ** -0.5, 0.0625, ((0, 128),))
    w_down = bell_draw(keys[11], (DEVICES, FF_SLICE, D), FF ** -0.5, 0.125, ((0, 128),))
    return {"queries": queries, "latent_cache": latent_cache, "lengths": lengths, "residual": residual, "w_uv": w_uv, "w_out": w_out, "norm_gain": norm_gain, "expert_ids": expert_ids, "gate_values": gate_values, "w_gate": w_gate, "w_up": w_up, "w_down": w_down}


score_scale = 192.0 ** (-0.5)
epsilon = 1e-06

def attend_one(inputs):
    query_row, cache_row, length = inputs
    scores = jnp.dot(query_row, cache_row.T, preferred_element_type=jnp.float32) * score_scale
    visible = jnp.arange(MAXLEN) < length
    scores = jnp.where(visible[None, :], scores, -jnp.inf)
    weights = jax.nn.softmax(scores, axis=-1).astype(jnp.bfloat16)
    return jnp.dot(weights, cache_row[:, :LAT], preferred_element_type=jnp.float32).astype(jnp.bfloat16)

def reference(queries, latent_cache, lengths, residual, w_uv, w_out, norm_gain, expert_ids, gate_values, w_gate, w_up, w_down):
    latent = lax.map(attend_one, (queries, latent_cache, lengths))
    latent = lax.optimization_barrier(latent)
    head_out = jnp.einsum('rhc,hcv->rhv', latent.astype(jnp.float32), w_uv.astype(jnp.float32)).astype(jnp.bfloat16)
    projected = jnp.dot(head_out.reshape(ROWS, HEADS * VHEAD), w_out, preferred_element_type=jnp.float32)
    attended = (residual.astype(jnp.float32) + projected).astype(jnp.bfloat16)
    attended = lax.optimization_barrier(attended)
    values = attended.astype(jnp.float32)
    mean_square = lax.optimization_barrier(jnp.mean(values * values, axis=-1, keepdims=True))
    normed = (values * lax.rsqrt(mean_square + epsilon) * norm_gain.astype(jnp.float32)).astype(jnp.bfloat16)
    normed = lax.optimization_barrier(normed)
    normed_wide = normed.astype(jnp.float32)
    gate_wide = gate_values.astype(jnp.float32)

    def add_expert(expert, total):
        start = (expert * SPLIT).astype(jnp.int32)
        gate_blocks = lax.dynamic_slice_in_dim(w_gate, start, SPLIT, 0).astype(jnp.float32)
        up_blocks = lax.dynamic_slice_in_dim(w_up, start, SPLIT, 0).astype(jnp.float32)
        down_blocks = lax.dynamic_slice_in_dim(w_down, start, SPLIT, 0).astype(jnp.float32)
        gate_part = jnp.einsum('rd,sdf->rsf', normed_wide, gate_blocks)
        up_part = jnp.einsum('rd,sdf->rsf', normed_wide, up_blocks)
        hidden = (jax.nn.silu(gate_part) * up_part).astype(jnp.bfloat16)
        hidden = lax.optimization_barrier(hidden)
        output = jnp.einsum('rsf,sfd->rd', hidden.astype(jnp.float32), down_blocks)
        weight = lax.optimization_barrier(jnp.sum(gate_wide * (expert_ids == expert), axis=1))
        return total + output * weight[:, None]
    total = lax.fori_loop(0, EXPERTS, add_expert, jnp.zeros((ROWS, D), jnp.float32))
    return (values + total).astype(jnp.bfloat16)
```

```python
import itertools

import jax
import jax.numpy as jnp
from jax import lax
from jax.sharding import PartitionSpec as P

EXPERTS = 16
AXES = ("role", "dev")
SIDE = 4
EXTRA = 128

score_scale = 192.0 ** (-0.5)
epsilon = 1e-06


def device_at(role, a, b, c):
    x, y, z = (a, b, c) if role == 0 else (b, c, a)
    return ((role * SIDE + x) * SIDE + y) * SIDE + z


def groups(along):
    rest = [axis for axis in "abc" if axis not in along]
    out = []
    for role in range(2):
        for fixed in itertools.product(range(SIDE), repeat=len(rest)):
            group = []
            for moving in itertools.product(range(SIDE), repeat=len(along)):
                at = dict(zip(rest, fixed))
                at.update(zip(along, moving))
                group.append(device_at(role, at["a"], at["b"], at["c"]))
            out.append(group)
    return out


def shift(value, axis, step):
    pairs = []
    for group in groups(axis):
        pairs += [(group[i], group[(i + step) % SIDE]) for i in range(SIDE)]
    return lax.ppermute(value, AXES, pairs)


def swap_cores(value):
    return lax.ppermute(value, "role", [(0, 1), (1, 0)])


def coordinates():
    role = lax.axis_index("role")
    dev = lax.axis_index("dev")
    x, y, z = dev // 16, dev // 4 % 4, dev % 4
    first = role == 0
    return role, jnp.where(first, x, z), jnp.where(first, y, x), jnp.where(first, z, y)


def part(value, at, count, axis):
    width = value.shape[axis] // count
    return lax.dynamic_slice_in_dim(value, at * width, width, axis)


def in_order(slots, mine):
    stacked = jnp.stack(slots)
    return jnp.take(stacked, (mine - jnp.arange(SIDE)) % SIDE, axis=0)


def on_device(
    queries,
    latent_cache,
    lengths,
    residual,
    w_uv,
    w_out,
    norm_gain,
    expert_ids,
    gate_values,
    w_gate,
    w_up,
    w_down,
):
    bf16, f32 = jnp.bfloat16, jnp.float32
    role, a, b, c = coordinates()
    latent_width = w_uv.shape[1]
    cache_length = latent_cache.shape[1]
    rows, width = residual.shape
    heads = queries.shape[1]
    block = width // SIDE

    named = expert_ids[:, :, None] == jnp.arange(EXPERTS)[None, None, :]
    weights = jnp.sum(jnp.where(named, gate_values[:, :, None].astype(f32), 0.0), axis=1)
    weights = jnp.pad(weights.astype(bf16), ((0, 0), (0, EXTRA - EXPERTS)))

    def bundle(step):
        to = (c + step) % SIDE
        return part(w_out, to, SIDE, 1), jnp.concatenate([part(residual, to, SIDE, 1), weights], 1)

    pooled_out, pooled_uv, pooled_rows = [], [], []
    for step in range(SIDE):
        out_part, row_part = bundle(step)
        if step:
            out_part, row_part = shift(out_part, "c", step), shift(row_part, "c", step)
        pooled_out.append(out_part)
        pooled_rows.append(row_part)
        pooled_uv.append(shift(w_uv[0], "c", step) if step else w_uv[0])
    out_weights = in_order(pooled_out, c).reshape(-1, block)
    uv_weights = in_order(pooled_uv, c)
    own_rows = in_order(pooled_rows, c)

    slot = jnp.arange(heads)
    ha, hb, hc = slot // 16, slot // 4 % 4, slot % 4
    head_at = jnp.where(role == 0, ha * 16 + hb * 4 + hc, hb * 16 + hc * 4 + ha)
    pick = (head_at[:, None] == jnp.arange(heads)[None, :]).astype(bf16)
    ordered = jnp.einsum("gh,rhc->rgc", pick, queries, preferred_element_type=f32).astype(bf16)

    scores = (
        jnp.einsum("rhc,rpc->rhp", ordered, latent_cache, preferred_element_type=f32) * score_scale
    )
    visible = (jnp.arange(cache_length)[None, :] < lengths[:, None])[:, None, :]
    scores = jnp.where(visible, scores, -jnp.inf)
    soft_weights = jax.nn.softmax(scores, axis=-1).astype(bf16)
    latent = jnp.einsum(
        "rhp,rpc->hrc", soft_weights, latent_cache[:, :, :latent_width], preferred_element_type=f32
    ).astype(bf16)
    sent = latent.reshape(16, SIDE * rows, latent_width)
    got = lax.all_to_all(sent, AXES, 0, 0, axis_index_groups=groups("ab"), tiled=True)
    got = got.reshape(16, SIDE, rows, latent_width)
    head_out = jnp.concatenate(
        [
            jnp.dot(
                got[:, s].reshape(16 * rows, latent_width), uv_weights[s], preferred_element_type=f32
            ).astype(bf16)
            for s in range(SIDE)
        ],
        axis=1,
    )
    gathered = in_order([head_out] + [shift(head_out, "c", s) for s in (1, 2, 3)], c)
    gathered = gathered.reshape(SIDE, SIDE, SIDE * rows, -1).transpose(1, 0, 2, 3)
    partial = jnp.einsum("acrk,kn->acrn", gathered, out_weights, preferred_element_type=f32)
    partial = jnp.pad(partial, ((0, 0), (0, 0), (0, 0), (0, EXTRA)))
    own = (jnp.arange(SIDE)[:, None] == a) & (jnp.arange(SIDE)[None, :] == b)
    partial = partial.reshape(SIDE, SIDE, SIDE, rows, -1) + jnp.where(
        own[:, None, :, None, None], own_rows.astype(f32)[None, :, None], 0.0
    )
    partial = partial.astype(bf16).reshape(SIDE, 16 * rows, -1)

    def block_of(value, at):
        return lax.dynamic_index_in_dim(value, at % SIDE, 0, keepdims=False)

    total = block_of(partial, a).astype(f32)
    for s in (1, 2, 3):
        total = total + shift(block_of(partial, a + s), "a", s).astype(f32)
    total = total.astype(bf16)
    summed = total.astype(f32)
    for s in (1, 2, 3):
        summed = summed + shift(total, "b", s).astype(f32)
    attended = summed.astype(bf16)
    columns = in_order([attended] + [shift(attended, "c", s) for s in (1, 2, 3)], c)
    weights = columns[0, :, block:]
    values = columns[:, :, :block].transpose(1, 0, 2).reshape(-1, width).astype(f32)
    mean_square = jnp.mean(values * values, axis=-1, keepdims=True)
    normed = (values * lax.rsqrt(mean_square + epsilon) * norm_gain.astype(f32)).astype(bf16)
    mine = lax.dynamic_slice_in_dim(values, (c * SIDE + b) * rows, rows, 0)

    told = jnp.concatenate([normed, weights], axis=1)
    core_rows = jnp.concatenate([told] + [shift(told, "a", s) for s in (1, 2, 3)], axis=0)
    all_rows = jnp.concatenate([core_rows, swap_cores(core_rows)], axis=0)

    my_expert = (role * 64 + lax.axis_index("dev")) // (128 // EXPERTS)
    chosen = (jnp.arange(EXTRA) == my_expert).astype(f32)
    row_weight = jnp.sum(all_rows[:, width:].astype(f32) * chosen, axis=1)
    inputs = all_rows[:, :width]
    gate_part = jnp.dot(inputs, w_gate[0], preferred_element_type=f32)
    up_part = jnp.dot(inputs, w_up[0], preferred_element_type=f32)
    hidden = (jax.nn.silu(gate_part) * up_part).astype(bf16)
    half = hidden.shape[0] // 2

    def down(at):
        span = slice(at * half, (at + 1) * half)
        return jnp.dot(hidden[span], w_down[0], preferred_element_type=f32) * row_weight[span, None]

    other = swap_cores(down(1).astype(bf16))
    sums = (down(0) + other.astype(f32)).astype(bf16).reshape(SIDE, 16 * rows, width)
    total = sums[0].astype(f32)
    for s in (1, 2, 3):
        total = total + shift(sums[s], "a", -s).astype(f32)
    last = total.astype(bf16).reshape(16, rows, width)
    last = lax.all_to_all(last, AXES, 0, 0, axis_index_groups=groups("cb"), tiled=True)
    combined = jnp.sum(last.astype(f32), axis=0)
    return (mine + combined).astype(bf16)


def solution(mesh):
    return jax.shard_map(
        on_device,
        mesh=mesh,
        in_specs=(
            P(("role", "dev"), None, None),
            P(("role", "dev"), None, None),
            P(("role", "dev")),
            P(("role", "dev"), None),
            P("dev", None, None),
            P("dev", None),
            P(),
            P(("role", "dev"), None),
            P(("role", "dev"), None),
            P(("role", "dev"), None, None),
            P(("role", "dev"), None, None),
            P(("role", "dev"), None, None),
        ),
        out_specs=P(("role", "dev"), None),
        check_vma=False,
    )
```

```python
import functools
import itertools

import jax
import jax.numpy as jnp
from jax import lax
from jax.experimental import pallas as pl
from jax.experimental.pallas import tpu as pltpu
from jax.sharding import PartitionSpec as P

EXPERTS = 16
AXES = ("role", "dev")
SIDE = 4
EXTRA = 128
GROUP = 16
CHUNK = 512

score_scale = 192.0 ** (-0.5)
epsilon = 1e-06
bf16, f32 = jnp.bfloat16, jnp.float32


def device_at(role, a, b, c):
    x, y, z = (a, b, c) if role == 0 else (c, a, b)
    return ((role * SIDE + x) * SIDE + y) * SIDE + z


def groups(along):
    rest = [axis for axis in "abc" if axis not in along]
    out = []
    for role in range(2):
        for fixed in itertools.product(range(SIDE), repeat=len(rest)):
            group = []
            for moving in itertools.product(range(SIDE), repeat=len(along)):
                at = dict(zip(rest, fixed))
                at.update(zip(along, moving))
                group.append(device_at(role, at["a"], at["b"], at["c"]))
            out.append(group)
    return out


def shift(value, axis, step):
    pairs = []
    for group in groups(axis):
        pairs += [(group[i], group[(i + step) % SIDE]) for i in range(SIDE)]
    return lax.ppermute(value, AXES, pairs)


def shifts(value, axis):
    got = {step: shift(value, axis, step) for step in (2, 1, 3)}
    return [value] + [got[step] for step in (1, 2, 3)]


def swap_cores(value):
    return lax.ppermute(value, "role", [(0, 1), (1, 0)])


def call(body, out_shape, args, flops, limit, **given):
    smem = pl.BlockSpec(memory_space=pltpu.SMEM)
    vmem = pl.BlockSpec(memory_space=pltpu.VMEM)
    if "grid" not in given and "grid_spec" not in given:
        given["in_specs"] = [smem] + [vmem] * (len(args) - 1)
        given["out_specs"] = jax.tree.map(lambda _: vmem, out_shape)
    moved = sum(x.size * x.dtype.itemsize for x in [*args, *jax.tree.leaves(out_shape)])
    return pl.pallas_call(
        body,
        out_shape=out_shape,
        compiler_params=pltpu.CompilerParams(vmem_limit_bytes=limit * 2**20),
        cost_estimate=pl.CostEstimate(flops=flops, bytes_accessed=moved, transcendentals=0),
        **given,
    )(*args)


def back(mine, step):
    return lax.rem(mine - step + SIDE, SIDE)


def ahead(mine, step):
    return lax.rem(mine + step, SIDE)


def lanes(at, width):
    return pl.ds(pl.multiple_of(at * width, width), width)


def iota(shape, axis):
    return lax.broadcasted_iota(jnp.int32, shape, axis)


def bundle_kernel(at, w_out, w_uv, residual, ids, gates, *outs):
    c = at[3]
    latent, depth = w_uv.shape[1], w_out.shape[0]
    rows, width = residual.shape
    block = width // SIDE
    weights = jnp.zeros((rows, EXTRA), f32)
    for k in range(ids.shape[1]):
        named = ids[:, k : k + 1] == iota((rows, EXTRA), 1)
        weights = weights + jnp.where(named, gates[:, k : k + 1].astype(f32), 0.0)
    spread = (iota((GROUP, rows), 0) == iota((GROUP, rows), 1)).astype(f32).astype(bf16)

    def place(value):
        return jnp.dot(spread, value, preferred_element_type=f32).astype(bf16)

    weights = place(weights.astype(bf16))
    for step, out in enumerate(outs):
        to = lanes(ahead(c, step), block)
        for k in range(latent // depth):
            out[:depth, k * depth : (k + 1) * depth] = w_uv[0, k * depth : (k + 1) * depth, :]
        out[:depth, latent:] = w_out[:, to]
        out[depth:, :block] = place(residual[:, to])
        out[depth:, block : block + EXTRA] = weights
        if latent > EXTRA:
            out[depth:, block + EXTRA :] = jnp.zeros((GROUP, latent - EXTRA), bf16)


def attend_kernel(lengths, at, query, cache, out, most, norm, mixed, placed):
    row, chunk = pl.program_id(0), pl.program_id(1)
    length = lengths[row]
    heads, latent = mixed.shape
    size = cache.shape[1]

    @pl.when((row == 0) & (chunk == 0))
    def _():
        placed[...] = jnp.zeros_like(placed)

    @pl.when(chunk == 0)
    def _():
        most[...] = jnp.full_like(most, -jnp.inf)
        norm[...] = jnp.zeros_like(norm)
        mixed[...] = jnp.zeros_like(mixed)

    @pl.when(chunk * size < length)
    def _():
        keys = cache[0]
        scores = score_scale * lax.dot_general(
            query[0], keys, (((1,), (1,)), ((), ())), preferred_element_type=f32
        )
        scores = jnp.where(chunk * size + iota(scores.shape, 1) < length, scores, -jnp.inf)
        highest = jnp.maximum(most[...], jnp.max(scores, axis=1, keepdims=True))
        fade = jnp.exp(most[...] - highest)
        shares = jnp.exp(scores - highest)
        most[...] = highest
        norm[...] = norm[...] * fade + jnp.sum(shares, axis=1, keepdims=True)
        mixed[...] = mixed[...] * fade + jnp.dot(
            shares.astype(bf16), keys[:, :latent], preferred_element_type=f32
        )

    @pl.when(chunk == pl.num_programs(1) - 1)
    def _():
        done = (mixed[...] / norm[...]).astype(bf16)
        line, head = iota((placed.shape[0], heads), 0), iota((placed.shape[0], heads), 1)
        a, b, c = line >> 6, (line >> 4) & 3, line & 3
        wanted = jnp.where(at[0] == 0, a * 16 + b * 4 + c, c * 16 + a * 4 + b)
        pick = ((wanted == head) & (((line >> 2) & 3) == row)).astype(f32).astype(bf16)
        placed[...] += jnp.dot(pick, done, preferred_element_type=f32)

        @pl.when(row == pl.num_programs(0) - 1)
        def _():
            out[...] = placed[...].astype(bf16)


def attend(lengths, at, queries, cache):
    rows, heads, width = queries.shape
    cache_length = cache.shape[1]
    size = min(CHUNK, cache_length)
    latent = width - 64
    lines = rows * heads
    grid_spec = pltpu.PrefetchScalarGridSpec(
        num_scalar_prefetch=2,
        grid=(rows, cache_length // size),
        in_specs=[
            pl.BlockSpec((1, heads, width), lambda r, k, lengths, at: (r, 0, 0)),
            pl.BlockSpec(
                (1, size, width),
                lambda r, k, lengths, at: (r, jnp.minimum(k, (lengths[r] - 1) // size), 0),
            ),
        ],
        out_specs=pl.BlockSpec((lines, latent), lambda r, k, lengths, at: (0, 0)),
        scratch_shapes=[
            pltpu.VMEM((heads, 1), f32),
            pltpu.VMEM((heads, 1), f32),
            pltpu.VMEM((heads, latent), f32),
            pltpu.VMEM((lines, latent), f32),
        ],
    )
    return call(
        attend_kernel,
        jax.ShapeDtypeStruct((lines, latent), bf16),
        (lengths, at, queries, cache),
        2 * lines * cache_length * (width + latent),
        16,
        grid_spec=grid_spec,
    )


def heads_kernel(at, latents, w0, w1, w2, w3, out):
    lines = latents.shape[0]
    depth, latent = w0.shape
    line = iota((lines, depth), 0)
    count = lines // SIDE
    gather = (iota((count, lines), 0) == (iota((count, lines), 1) >> 2)).astype(f32).astype(bf16)
    for step, w in enumerate((w0, w1, w2, w3)):
        head = back(at[3], step)
        value = jnp.zeros((lines, depth), f32)
        for k in range(latent // depth):
            span = slice(k * depth, (k + 1) * depth)
            value = value + jnp.dot(latents[:, span], w[:, span], preferred_element_type=f32)
        value = jnp.where((line & 3) == head, value, 0.0).astype(bf16)
        out[head] = jnp.dot(gather, value, preferred_element_type=f32).astype(bf16)


def project_kernel(at, h0, h1, h2, h3, p0, p1, p2, p3, o0, o1, o2, o3, lines):
    packs = (p0, p1, p2, p3)
    heads, _, depth = h0.shape
    block = o0.shape[1] - EXTRA
    latent = p0.shape[1] - block
    a, b, c = at[1], at[2], at[3]
    for step in range(SIDE):
        rows = pl.ds(pl.multiple_of(ahead(a, step) * GROUP, GROUP), GROUP)
        for j, h in enumerate((h0, h1, h2, h3)):
            for k in range(heads):
                lines[step, back(c, j), :, k * depth : (k + 1) * depth] = h[back(c, k), rows, :]
    for step, out in enumerate((o0, o1, o2, o3)):
        left = lines[step].reshape(SIDE * GROUP, heads * depth)
        total = jnp.zeros((SIDE * GROUP, block), f32)
        for k, pack in enumerate(packs):
            total = total + jnp.dot(
                left[:, k * depth : (k + 1) * depth],
                pack[:depth, latent:],
                preferred_element_type=f32,
            )
        out[:, :block] = total.astype(bf16)
        out[:, block:] = jnp.zeros((SIDE * GROUP, EXTRA), bf16)
    move = iota((GROUP, GROUP), 0) == b * 4 + iota((GROUP, GROUP), 1)
    move = (move & (iota((GROUP, GROUP), 1) < 4)).astype(f32).astype(bf16)
    for j, pack in enumerate(packs):
        rows = pl.ds(pl.multiple_of(back(c, j) * GROUP, GROUP), GROUP)
        own = jnp.dot(move, pack[depth:, : block + EXTRA], preferred_element_type=f32)
        o0[rows, :] = (o0[rows, :].astype(f32) + own).astype(bf16)


def norm_kernel(at, s0, s1, s2, s3, gain, out, mine):
    slots = (s0, s1, s2, s3)
    width = gain.shape[1]
    block = width // SIDE
    squares = 0.0
    for slot in slots:
        value = slot[:, :block].astype(f32)
        squares = squares + jnp.sum(value * value, axis=1, keepdims=True)
    factor = lax.rsqrt(squares * (1.0 / width) + epsilon)
    rows = pl.ds(pl.multiple_of(at[3] * GROUP, GROUP), GROUP)
    for step, slot in enumerate(slots):
        to = lanes(back(at[3], step), block)
        out[:, to] = (slot[:, :block].astype(f32) * factor * gain[:, to]).astype(bf16)
        mine[:, to] = slot[rows, :block]
    out[:, width:] = s0[:, block:]


def experts_kernel(count, parts, at, *refs):
    xs, ws, refs = refs[:count], refs[count : 2 * count], refs[2 * count :]
    gates, ups, downs, refs = refs[0:2], refs[2:4], refs[4:6], refs[6:]
    outs, (gate_sum, up_sum, hidden, weights) = refs[:count], refs[count:]
    step = pl.program_id(0)
    units = gates[0].shape[2]
    rows = xs[0].shape[0]

    def joined(refs):
        return refs[0][...] if count == 1 else jnp.concatenate([r[...] for r in refs], axis=0)

    @pl.when(step < parts)
    def _():
        x = joined(xs)
        for k in range(2):
            span = slice(k * units, (k + 1) * units)
            gate = jnp.dot(x, gates[k][0], preferred_element_type=f32)
            up = jnp.dot(x, ups[k][0], preferred_element_type=f32)

            @pl.when(step == 0)
            def _():
                gate_sum[:, span] = gate
                up_sum[:, span] = up

            @pl.when(step > 0)
            def _():
                gate_sum[:, span] += gate
                up_sum[:, span] += up

    @pl.when(step == parts - 1)
    def _():
        gate = gate_sum[...]
        hidden[...] = (gate * (1.0 / (1.0 + jnp.exp(-gate))) * up_sum[...]).astype(bf16)
        told = joined(ws).astype(f32)
        for k in range(2):
            chosen = iota(told.shape, 1) == at[4 + k]
            weight = jnp.sum(jnp.where(chosen, told, 0.0), axis=1, keepdims=True)
            weights[k] = jnp.broadcast_to(weight, told.shape)

    @pl.when(step >= parts)
    def _():
        total = 0.0
        for k in range(2):
            value = jnp.dot(
                hidden[:, k * units : (k + 1) * units], downs[k][0], preferred_element_type=f32
            )
            total = total + value * weights[k][:, 0:1]
        for k, out in enumerate(outs):
            out[...] = total[k * rows : (k + 1) * rows].astype(bf16)


def experts(at, slots, gates, ups, downs):
    count, parts = len(slots), SIDE
    rows = slots[0].shape[0]
    width, units = gates[0].shape[1:]
    block = width // parts

    def first(i):
        return jnp.minimum(i, parts - 1)

    def second(i):
        return jnp.maximum(i - parts, 0)

    in_specs = [pl.BlockSpec(memory_space=pltpu.SMEM)]
    in_specs += [pl.BlockSpec((rows, block), lambda i: (0, first(i)))] * count
    in_specs += [pl.BlockSpec((rows, EXTRA), lambda i: (0, width // EXTRA))] * count
    in_specs += [pl.BlockSpec((1, block, units), lambda i: (0, first(i), 0))] * 4
    in_specs += [pl.BlockSpec((1, units, block), lambda i: (0, 0, second(i)))] * 2
    return call(
        functools.partial(experts_kernel, count, parts),
        [jax.ShapeDtypeStruct((rows, width), bf16)] * count,
        (at, *slots, *slots, *gates, *ups, *downs),
        12 * count * rows * width * units,
        24,
        grid=(2 * parts,),
        in_specs=in_specs,
        out_specs=[pl.BlockSpec((rows, block), lambda i: (0, second(i)))] * count,
        scratch_shapes=[
            pltpu.VMEM((count * rows, 2 * units), f32),
            pltpu.VMEM((count * rows, 2 * units), f32),
            pltpu.VMEM((count * rows, 2 * units), bf16),
            pltpu.VMEM((2, count * rows, EXTRA), f32),
        ],
    )


def on_device(
    queries,
    latent_cache,
    lengths,
    residual,
    w_uv,
    w_out,
    norm_gain,
    expert_ids,
    gate_values,
    w_gate,
    w_up,
    w_down,
):
    role, dev = lax.axis_index("role"), lax.axis_index("dev")
    x, y, z = dev // 16, dev // 4 % 4, dev % 4
    first = role == 0
    a, b, c = jnp.where(first, x, y), jnp.where(first, y, z), jnp.where(first, z, x)
    per_expert = 128 // EXPERTS
    experts_here = [(role * 64 + dev) // per_expert, ((1 - role) * 64 + dev) // per_expert]
    at = jnp.stack([role, a, b, c, *experts_here, role, role]).astype(jnp.int32)
    rows, width = residual.shape
    latent, depth = w_uv.shape[1:]
    block = width // SIDE
    count = GROUP * SIDE

    shape = jax.ShapeDtypeStruct((depth + GROUP, latent + block), bf16)
    packs = call(
        bundle_kernel,
        [shape] * SIDE,
        (at, w_out, w_uv, residual, expert_ids, gate_values),
        0,
        16,
    )
    packs = [packs[0]] + [shift(packs[s], "c", s) for s in (1, 2, 3)]
    gates, ups, downs = [(w, swap_cores(w)) for w in (w_gate, w_up, w_down)]

    sent = attend(lengths, at, queries, latent_cache).reshape(16, SIDE * rows, latent)
    got = lax.all_to_all(sent, AXES, 0, 0, axis_index_groups=groups("ab"), tiled=True)
    got = got.reshape(-1, latent)
    vmem = pl.BlockSpec(memory_space=pltpu.VMEM)
    head_out = call(
        heads_kernel,
        jax.ShapeDtypeStruct((SIDE, count, depth), bf16),
        (at, got, *packs),
        2 * SIDE * got.size * depth,
        16,
        grid=(1,),
        in_specs=[pl.BlockSpec(memory_space=pltpu.SMEM), vmem]
        + [pl.BlockSpec((depth, latent), lambda i: (0, 0))] * SIDE,
        out_specs=vmem,
    )
    gathered = shifts(head_out, "c")
    partial = call(
        project_kernel,
        [jax.ShapeDtypeStruct((count, block + EXTRA), bf16)] * SIDE,
        (at, *gathered, *packs),
        2 * SIDE * count * SIDE * depth * block,
        24,
        scratch_shapes=[pltpu.VMEM((SIDE, SIDE, GROUP, SIDE * depth), bf16)],
    )

    def added(parts):
        return functools.reduce(lambda u, v: u + v, [p.astype(f32) for p in parts]).astype(bf16)

    total = added([partial[0]] + [shift(partial[s], "a", s) for s in (2, 1, 3)])
    attended = added(shifts(total, "b"))
    columns = shifts(attended, "c")
    normed, mine = call(
        norm_kernel,
        [
            jax.ShapeDtypeStruct((count, width + EXTRA), bf16),
            jax.ShapeDtypeStruct((GROUP, width), bf16),
        ],
        (at, *columns, norm_gain.astype(f32).reshape(1, width)),
        0,
        16,
    )

    near = [shift(normed, "a", s) for s in (1, 3)]
    far = shift(normed, "a", 2)
    run = functools.partial(experts, at, gates=gates, ups=ups, downs=downs)
    (own_sum,) = run([normed])
    near_sums = run(near)
    (far_sum,) = run([far])
    sums = [shift(near_sums[0], "a", -1), shift(near_sums[1], "a", -3), shift(far_sum, "a", -2)]
    last = added([own_sum] + sums).reshape(16, rows, width)
    last = lax.all_to_all(last, AXES, 0, 0, axis_index_groups=groups("cb"), tiled=True)
    combined = jnp.sum(last.astype(f32), axis=0)
    mine = lax.dynamic_slice_in_dim(mine, b * rows, rows, 0)
    return (mine.astype(f32) + combined).astype(bf16)


def solution(mesh):
    return jax.shard_map(
        on_device,
        mesh=mesh,
        in_specs=(
            P(("role", "dev"), None, None),
            P(("role", "dev"), None, None),
            P(("role", "dev")),
            P(("role", "dev"), None),
            P("dev", None, None),
            P("dev", None),
            P(),
            P(("role", "dev"), None),
            P(("role", "dev"), None),
            P(("role", "dev"), None, None),
            P(("role", "dev"), None, None),
            P(("role", "dev"), None, None),
        ),
        out_specs=P(("role", "dev"), None),
        check_vma=False,
    )
```

```python
import functools
import itertools

import jax
import jax.numpy as jnp
from jax import lax
from jax.experimental import pallas as pl
from jax.experimental.pallas import tpu as pltpu
from jax.sharding import PartitionSpec as P

EXPERTS = 16
AXES = ("role", "dev")
SIDE = 4
EXTRA = 128
GROUP = 16
CHUNK = 1024

score_scale = 192.0 ** (-0.5)
epsilon = 1e-06
bf16, f32 = jnp.bfloat16, jnp.float32


def device_at(role, a, b, c):
    x, y, z = (a, b, c) if role == 0 else (c, a, b)
    return ((role * SIDE + x) * SIDE + y) * SIDE + z


def groups(along):
    rest = [axis for axis in "abc" if axis not in along]
    out = []
    for role in range(2):
        for fixed in itertools.product(range(SIDE), repeat=len(rest)):
            group = []
            for moving in itertools.product(range(SIDE), repeat=len(along)):
                at = dict(zip(rest, fixed))
                at.update(zip(along, moving))
                group.append(device_at(role, at["a"], at["b"], at["c"]))
            out.append(group)
    return out


def shift(value, axis, step):
    pairs = []
    for group in groups(axis):
        pairs += [(group[i], group[(i + step) % SIDE]) for i in range(SIDE)]
    return lax.ppermute(value, AXES, pairs)


def shifts(value, axis):
    got = {step: shift(value, axis, step) for step in (2, 1, 3)}
    return [value] + [got[step] for step in (1, 2, 3)]


def swap_cores(value):
    return lax.ppermute(value, "role", [(0, 1), (1, 0)])


def call(body, out_shape, args, flops, limit, **given):
    smem = pl.BlockSpec(memory_space=pltpu.SMEM)
    vmem = pl.BlockSpec(memory_space=pltpu.VMEM)
    if "in_specs" not in given:
        given["in_specs"] = [smem] + [vmem] * (len(args) - 1)
        given["out_specs"] = jax.tree.map(lambda _: vmem, out_shape)
    moved = sum(x.size * x.dtype.itemsize for x in [*args, *jax.tree.leaves(out_shape)])
    return pl.pallas_call(
        body,
        out_shape=out_shape,
        compiler_params=pltpu.CompilerParams(vmem_limit_bytes=limit * 2**20),
        cost_estimate=pl.CostEstimate(
            flops=flops, bytes_accessed=moved if flops else 0, transcendentals=0
        ),
        **given,
    )(*args)


def back(mine, step):
    return lax.rem(mine - step + SIDE, SIDE)


def ahead(mine, step):
    return lax.rem(mine + step, SIDE)


def lanes(at, width):
    return pl.ds(pl.multiple_of(at * width, width), width)


def iota(shape, axis):
    return lax.broadcasted_iota(jnp.int32, shape, axis)


def bundle_kernel(at, w_out, w_uv, residual, ids, gates, *outs):
    c = at[3]
    latent, depth = w_uv.shape[1], w_out.shape[0]
    rows, width = residual.shape
    block = width // SIDE
    weights = jnp.zeros((rows, EXTRA), f32)
    for k in range(ids.shape[1]):
        named = ids[:, k : k + 1] == iota((rows, EXTRA), 1)
        weights = weights + jnp.where(named, gates[:, k : k + 1].astype(f32), 0.0)
    spread = (iota((GROUP, rows), 0) == iota((GROUP, rows), 1)).astype(f32).astype(bf16)

    def place(value):
        return jnp.dot(spread, value, preferred_element_type=f32).astype(bf16)

    weights = place(weights.astype(bf16))
    for step, out in enumerate(outs):
        to = lanes(ahead(c, step), block)
        for k in range(latent // depth):
            out[:depth, k * depth : (k + 1) * depth] = w_uv[0, k * depth : (k + 1) * depth, :]
        out[:depth, latent:] = w_out[:, to]
        out[depth:, :block] = place(residual[:, to])
        out[depth:, block : block + EXTRA] = weights
        if latent > EXTRA:
            out[depth:, block + EXTRA :] = jnp.zeros((GROUP, latent - EXTRA), bf16)


def attend_kernel(lengths, at, query, cache, out, held, scores, most, norm, mixed, sems):
    rows, heads, _ = query.shape
    latent = mixed.shape[2]
    size = most.shape[2]
    parts = cache.shape[2] // size

    def copy(row, part):
        span = pl.ds(part * size, size)
        return pltpu.make_async_copy(
            cache.at[row, :, span], held.at[row, :, span], sems.at[row, part]
        )

    def where_live(step):
        for row in range(rows):
            for part in range(parts):
                act = functools.partial(step, row, part)
                if part:
                    pl.when(part * size < lengths[row])(act)
                else:
                    act()

    def score(row, part):
        span = slice(part * size, (part + 1) * size)
        copy(row, part).wait()
        value = score_scale * jnp.dot(query[row], held[row, :, span], preferred_element_type=f32)
        live = part * size + iota(value.shape, 1) < lengths[row]
        value = jnp.where(live, value, -jnp.inf)
        scores[row, :, span] = value
        most[row] = jnp.maximum(most[row], value) if part else value

    where_live(lambda row, part: copy(row, part).start())
    where_live(score)
    tops = [jnp.max(most[row], axis=1, keepdims=True) for row in range(rows)]

    def mix(row, part):
        span = slice(part * size, (part + 1) * size)
        shares = jnp.exp(scores[row, :, span] - tops[row])
        norm[row] = norm[row] + shares if part else shares
        value = lax.dot_general(
            shares.astype(bf16),
            held[row, :latent, span],
            (((1,), (1,)), ((), ())),
            preferred_element_type=f32,
        )
        mixed[row] = mixed[row] + value if part else value

    where_live(mix)
    lines = out.shape[0]
    line, head = iota((lines, heads), 0), iota((lines, heads), 1)
    a, b, c = line >> 6, (line >> 4) & 3, line & 3
    wanted = jnp.where(at[0] == 0, a * 16 + b * 4 + c, c * 16 + a * 4 + b)
    placed = jnp.zeros((lines, latent), f32)
    for row in range(rows):
        done = (mixed[row] / jnp.sum(norm[row], axis=1, keepdims=True)).astype(bf16)
        pick = ((wanted == head) & (((line >> 2) & 3) == row)).astype(f32).astype(bf16)
        placed = placed + jnp.dot(pick, done, preferred_element_type=f32)
    out[...] = placed.astype(bf16)


def attend(lengths, at, queries, cache):
    rows, heads, width = queries.shape
    cache_length = cache.shape[2]
    size = min(CHUNK, cache_length)
    latent = width - 64
    lines = rows * heads
    smem = pl.BlockSpec(memory_space=pltpu.SMEM)
    vmem = pl.BlockSpec(memory_space=pltpu.VMEM)
    return call(
        attend_kernel,
        jax.ShapeDtypeStruct((lines, latent), bf16),
        (lengths, at, queries, cache),
        2 * lines * cache_length * (width + latent),
        56,
        in_specs=[smem, smem, vmem, pl.BlockSpec(memory_space=pltpu.HBM)],
        out_specs=vmem,
        scratch_shapes=[
            pltpu.VMEM(cache.shape, bf16),
            pltpu.VMEM((rows, heads, cache_length), f32),
            pltpu.VMEM((rows, heads, size), f32),
            pltpu.VMEM((rows, heads, size), f32),
            pltpu.VMEM((rows, heads, latent), f32),
            pltpu.SemaphoreType.DMA((rows, cache_length // size)),
        ],
    )


def heads_kernel(at, latents, w0, w1, w2, w3, out):
    lines = latents.shape[0]
    depth, latent = w0.shape
    line = iota((lines, depth), 0)
    count = lines // SIDE
    gather = (iota((count, lines), 0) == (iota((count, lines), 1) >> 2)).astype(f32).astype(bf16)
    for step, w in enumerate((w0, w1, w2, w3)):
        head = back(at[3], step)
        value = jnp.zeros((lines, depth), f32)
        for k in range(latent // depth):
            span = slice(k * depth, (k + 1) * depth)
            value = value + jnp.dot(latents[:, span], w[:, span], preferred_element_type=f32)
        value = jnp.where((line & 3) == head, value, 0.0).astype(bf16)
        out[head] = jnp.dot(gather, value, preferred_element_type=f32).astype(bf16)


def project_kernel(at, h0, h1, h2, h3, p0, p1, p2, p3, o0, o1, o2, o3, lines):
    packs = (p0, p1, p2, p3)
    heads, _, depth = h0.shape
    block = o0.shape[1] - EXTRA
    latent = p0.shape[1] - block
    a, b, c = at[1], at[2], at[3]
    for step in range(SIDE):
        rows = pl.ds(pl.multiple_of(ahead(a, step) * GROUP, GROUP), GROUP)
        for j, h in enumerate((h0, h1, h2, h3)):
            for k in range(heads):
                lines[step, back(c, j), :, k * depth : (k + 1) * depth] = h[back(c, k), rows, :]
    for step, out in enumerate((o0, o1, o2, o3)):
        left = lines[step].reshape(SIDE * GROUP, heads * depth)
        total = jnp.zeros((SIDE * GROUP, block), f32)
        for k, pack in enumerate(packs):
            total = total + jnp.dot(
                left[:, k * depth : (k + 1) * depth],
                pack[:depth, latent:],
                preferred_element_type=f32,
            )
        out[:, :block] = total.astype(bf16)
        out[:, block:] = jnp.zeros((SIDE * GROUP, EXTRA), bf16)
    move = iota((GROUP, GROUP), 0) == b * 4 + iota((GROUP, GROUP), 1)
    move = (move & (iota((GROUP, GROUP), 1) < 4)).astype(f32).astype(bf16)
    for j, pack in enumerate(packs):
        rows = pl.ds(pl.multiple_of(back(c, j) * GROUP, GROUP), GROUP)
        own = jnp.dot(move, pack[depth:, : block + EXTRA], preferred_element_type=f32)
        o0[rows, :] = (o0[rows, :].astype(f32) + own).astype(bf16)


def norm_kernel(at, s0, s1, s2, s3, gain, out, mine):
    slots = (s0, s1, s2, s3)
    width = gain.shape[1]
    block = width // SIDE
    squares = 0.0
    for slot in slots:
        value = slot[:, :block].astype(f32)
        squares = squares + jnp.sum(value * value, axis=1, keepdims=True)
    factor = lax.rsqrt(squares * (1.0 / width) + epsilon)
    rows = pl.ds(pl.multiple_of(at[3] * GROUP, GROUP), GROUP)
    for step, slot in enumerate(slots):
        to = lanes(back(at[3], step), block)
        out[:, to] = (slot[:, :block].astype(f32) * factor * gain[:, to]).astype(bf16)
        mine[:, to] = slot[rows, :block]
    out[:, width:] = s0[:, block:]


def experts_kernel(count, parts, at, *refs):
    xs, ws, refs = refs[:count], refs[count : 2 * count], refs[2 * count :]
    gates, ups, downs, refs = refs[0:2], refs[2:4], refs[4:6], refs[6:]
    outs, (gate_sum, up_sum, hidden, weights) = refs[:count], refs[count:]
    step = pl.program_id(0)
    units = gates[0].shape[2]
    rows = xs[0].shape[0]

    def joined(refs):
        return refs[0][...] if count == 1 else jnp.concatenate([r[...] for r in refs], axis=0)

    @pl.when(step < parts)
    def _():
        x = joined(xs)
        for k in range(2):
            span = slice(k * units, (k + 1) * units)
            gate = jnp.dot(x, gates[k][0], preferred_element_type=f32)
            up = jnp.dot(x, ups[k][0], preferred_element_type=f32)

            @pl.when(step == 0)
            def _():
                gate_sum[:, span] = gate
                up_sum[:, span] = up

            @pl.when(step > 0)
            def _():
                gate_sum[:, span] += gate
                up_sum[:, span] += up

    @pl.when(step == parts - 1)
    def _():
        gate = gate_sum[...]
        hidden[...] = (gate * (1.0 / (1.0 + jnp.exp(-gate))) * up_sum[...]).astype(bf16)
        told = joined(ws).astype(f32)
        for k in range(2):
            chosen = iota(told.shape, 1) == at[4 + k]
            weight = jnp.sum(jnp.where(chosen, told, 0.0), axis=1, keepdims=True)
            weights[k] = jnp.broadcast_to(weight, told.shape)

    @pl.when(step >= parts)
    def _():
        total = 0.0
        for k in range(2):
            value = jnp.dot(
                hidden[:, k * units : (k + 1) * units], downs[k][0], preferred_element_type=f32
            )
            total = total + value * weights[k][:, 0:1]
        for k, out in enumerate(outs):
            out[...] = total[k * rows : (k + 1) * rows].astype(bf16)


def experts(at, slots, gates, ups, downs):
    count, parts = len(slots), SIDE
    rows = slots[0].shape[0]
    width, units = gates[0].shape[1:]
    block = width // parts

    def first(i):
        return jnp.minimum(i, parts - 1)

    def second(i):
        return jnp.maximum(i - parts, 0)

    in_specs = [pl.BlockSpec(memory_space=pltpu.SMEM)]
    in_specs += [pl.BlockSpec((rows, block), lambda i: (0, first(i)))] * count
    in_specs += [pl.BlockSpec((rows, EXTRA), lambda i: (0, width // EXTRA))] * count
    in_specs += [pl.BlockSpec((1, block, units), lambda i: (0, first(i), 0))] * 4
    in_specs += [pl.BlockSpec((1, units, block), lambda i: (0, 0, second(i)))] * 2
    return call(
        functools.partial(experts_kernel, count, parts),
        [jax.ShapeDtypeStruct((rows, width), bf16)] * count,
        (at, *slots, *slots, *gates, *ups, *downs),
        12 * count * rows * width * units,
        24,
        grid=(2 * parts,),
        in_specs=in_specs,
        out_specs=[pl.BlockSpec((rows, block), lambda i: (0, second(i)))] * count,
        scratch_shapes=[
            pltpu.VMEM((count * rows, 2 * units), f32),
            pltpu.VMEM((count * rows, 2 * units), f32),
            pltpu.VMEM((count * rows, 2 * units), bf16),
            pltpu.VMEM((2, count * rows, EXTRA), f32),
        ],
    )


def on_device(
    queries,
    latent_cache,
    lengths,
    residual,
    w_uv,
    w_out,
    norm_gain,
    expert_ids,
    gate_values,
    w_gate,
    w_up,
    w_down,
):
    role, dev = lax.axis_index("role"), lax.axis_index("dev")
    x, y, z = dev // 16, dev // 4 % 4, dev % 4
    first = role == 0
    a, b, c = jnp.where(first, x, y), jnp.where(first, y, z), jnp.where(first, z, x)
    per_expert = 128 // EXPERTS
    experts_here = [(role * 64 + dev) // per_expert, ((1 - role) * 64 + dev) // per_expert]
    at = jnp.stack([role, a, b, c, *experts_here, role, role]).astype(jnp.int32)
    rows, width = residual.shape
    latent, depth = w_uv.shape[1:]
    block = width // SIDE
    count = GROUP * SIDE

    shape = jax.ShapeDtypeStruct((depth + GROUP, latent + block), bf16)
    packs = call(
        bundle_kernel,
        [shape] * SIDE,
        (at, w_out, w_uv, residual, expert_ids, gate_values),
        0,
        60,
        grid=(1,),
        in_specs=[pl.BlockSpec(memory_space=pltpu.SMEM)]
        + [
            pl.BlockSpec(v.shape, lambda i, n=v.ndim: (0,) * n)
            for v in (w_out, w_uv, residual, expert_ids, gate_values)
        ],
        out_specs=[pl.BlockSpec(shape.shape, lambda i: (0, 0))] * SIDE,
    )
    packs = [packs[0]] + [shift(packs[s], "c", s) for s in (1, 2, 3)]
    gates, ups, downs = [(w, swap_cores(w)) for w in (w_gate, w_up, w_down)]

    sent = attend(lengths, at, queries, latent_cache.swapaxes(1, 2)).reshape(16, SIDE * rows, latent)
    got = lax.all_to_all(sent, AXES, 0, 0, axis_index_groups=groups("ab"), tiled=True)
    got, gates, ups, downs = lax.optimization_barrier((got, gates, ups, downs))
    got = got.reshape(-1, latent)
    vmem = pl.BlockSpec(memory_space=pltpu.VMEM)
    head_out = call(
        heads_kernel,
        jax.ShapeDtypeStruct((SIDE, count, depth), bf16),
        (at, got, *packs),
        2 * SIDE * got.size * depth,
        16,
        grid=(1,),
        in_specs=[pl.BlockSpec(memory_space=pltpu.SMEM), vmem]
        + [pl.BlockSpec((depth, latent), lambda i: (0, 0))] * SIDE,
        out_specs=vmem,
    )
    gathered = shifts(head_out, "c")
    partial = call(
        project_kernel,
        [jax.ShapeDtypeStruct((count, block + EXTRA), bf16)] * SIDE,
        (at, *gathered, *packs),
        2 * SIDE * count * SIDE * depth * block,
        24,
        scratch_shapes=[pltpu.VMEM((SIDE, SIDE, GROUP, SIDE * depth), bf16)],
    )

    def added(parts):
        return functools.reduce(lambda u, v: u + v, [p.astype(f32) for p in parts]).astype(bf16)

    total = added([partial[0]] + [shift(partial[s], "a", s) for s in (2, 1, 3)])
    attended = added(shifts(total, "b"))
    columns = shifts(attended, "c")
    normed, mine = call(
        norm_kernel,
        [
            jax.ShapeDtypeStruct((count, width + EXTRA), bf16),
            jax.ShapeDtypeStruct((GROUP, width), bf16),
        ],
        (at, *columns, norm_gain.astype(f32).reshape(1, width)),
        0,
        16,
    )

    near = [shift(normed, "a", s) for s in (1, 3)]
    far = shift(normed, "a", 2)
    run = functools.partial(experts, at, gates=gates, ups=ups, downs=downs)
    (own_sum,) = run([normed])
    near_sums = run(near)
    (far_sum,) = run([far])
    sums = [shift(near_sums[0], "a", -1), shift(near_sums[1], "a", -3), shift(far_sum, "a", -2)]
    last = added([own_sum] + sums).reshape(16, rows, width)
    last = lax.all_to_all(last, AXES, 0, 0, axis_index_groups=groups("cb"), tiled=True)
    combined = jnp.sum(last.astype(f32), axis=0)
    mine = lax.dynamic_slice_in_dim(mine, b * rows, rows, 0)
    return (mine.astype(f32) + combined).astype(bf16)


def solution(mesh):
    return jax.shard_map(
        on_device,
        mesh=mesh,
        in_specs=(
            P(("role", "dev"), None, None),
            P(("role", "dev"), None, None),
            P(("role", "dev")),
            P(("role", "dev"), None),
            P("dev", None, None),
            P("dev", None),
            P(),
            P(("role", "dev"), None),
            P(("role", "dev"), None),
            P(("role", "dev"), None, None),
            P(("role", "dev"), None, None),
            P(("role", "dev"), None, None),
        ),
        out_specs=P(("role", "dev"), None),
        check_vma=False,
    )
```

```python
import functools
import itertools

import jax
import jax.numpy as jnp
from jax import lax
from jax.experimental import pallas as pl
from jax.experimental.pallas import tpu as pltpu
from jax.sharding import PartitionSpec as P

EXPERTS = 16
AXES = ("role", "dev")
SIDE = 4
EXTRA = 128
GROUP = 16
CHUNK = 1024

score_scale = 192.0 ** (-0.5)
epsilon = 1e-06
bf16, f32 = jnp.bfloat16, jnp.float32


def device_at(role, a, b, c):
    x, y, z = (a, b, c) if role == 0 else (c, a, b)
    return ((role * SIDE + x) * SIDE + y) * SIDE + z


def groups(along):
    rest = [axis for axis in "abc" if axis not in along]
    out = []
    for role in range(2):
        for fixed in itertools.product(range(SIDE), repeat=len(rest)):
            group = []
            for moving in itertools.product(range(SIDE), repeat=len(along)):
                at = dict(zip(rest, fixed))
                at.update(zip(along, moving))
                group.append(device_at(role, at["a"], at["b"], at["c"]))
            out.append(group)
    return out


def shift(value, axis, step):
    pairs = []
    for group in groups(axis):
        pairs += [(group[i], group[(i + step) % SIDE]) for i in range(SIDE)]
    return lax.ppermute(value, AXES, pairs)


def shifts(value, axis):
    got = {step: shift(value, axis, step) for step in (2, 1, 3)}
    return [value] + [got[step] for step in (1, 2, 3)]


def swap_cores(value):
    return lax.ppermute(value, "role", [(0, 1), (1, 0)])


def call(body, out_shape, args, flops, limit, **given):
    smem = pl.BlockSpec(memory_space=pltpu.SMEM)
    vmem = pl.BlockSpec(memory_space=pltpu.VMEM)
    if "in_specs" not in given:
        given["in_specs"] = [smem] + [vmem] * (len(args) - 1)
        given["out_specs"] = jax.tree.map(lambda _: vmem, out_shape)
    moved = sum(x.size * x.dtype.itemsize for x in [*args, *jax.tree.leaves(out_shape)])
    return pl.pallas_call(
        body,
        out_shape=out_shape,
        compiler_params=pltpu.CompilerParams(vmem_limit_bytes=limit * 2**20),
        cost_estimate=pl.CostEstimate(
            flops=flops, bytes_accessed=moved if flops else 0, transcendentals=0
        ),
        **given,
    )(*args)


def back(mine, step):
    return lax.rem(mine - step + SIDE, SIDE)


def ahead(mine, step):
    return lax.rem(mine + step, SIDE)


def lanes(at, width):
    return pl.ds(pl.multiple_of(at * width, width), width)


def iota(shape, axis):
    return lax.broadcasted_iota(jnp.int32, shape, axis)


def bundle_kernel(at, w_out, w_uv, residual, ids, gates, *outs):
    c = at[3]
    latent, depth = w_uv.shape[1], w_out.shape[0]
    rows, width = residual.shape
    block = width // SIDE
    weights = jnp.zeros((rows, EXTRA), f32)
    for k in range(ids.shape[1]):
        named = ids[:, k : k + 1] == iota((rows, EXTRA), 1)
        weights = weights + jnp.where(named, gates[:, k : k + 1].astype(f32), 0.0)
    spread = (iota((GROUP, rows), 0) == iota((GROUP, rows), 1)).astype(f32).astype(bf16)

    def place(value):
        return jnp.dot(spread, value, preferred_element_type=f32).astype(bf16)

    weights = place(weights.astype(bf16))
    for step, out in enumerate(outs):
        to = lanes(ahead(c, step), block)
        for k in range(latent // depth):
            out[:depth, k * depth : (k + 1) * depth] = w_uv[0, k * depth : (k + 1) * depth, :]
        out[:depth, latent:] = w_out[:, to]
        out[depth:, :block] = place(residual[:, to])
        out[depth:, block : block + EXTRA] = weights
        if latent > EXTRA:
            out[depth:, block + EXTRA :] = jnp.zeros((GROUP, latent - EXTRA), bf16)


def attend_kernel(lengths, at, query, cache, out, held, scores, most, norm, mixed, sems):
    rows, heads, _ = query.shape
    latent = mixed.shape[2]
    size = most.shape[2]
    parts = cache.shape[2] // size

    def copy(row, part):
        span = pl.ds(part * size, size)
        return pltpu.make_async_copy(
            cache.at[row, :, span], held.at[row, :, span], sems.at[row, part]
        )

    def where_live(step):
        for row in range(rows):
            for part in range(parts):
                act = functools.partial(step, row, part)
                if part:
                    pl.when(part * size < lengths[row])(act)
                else:
                    act()

    def score(row, part):
        span = slice(part * size, (part + 1) * size)
        copy(row, part).wait()
        value = score_scale * jnp.dot(query[row], held[row, :, span], preferred_element_type=f32)
        live = part * size + iota(value.shape, 1) < lengths[row]
        value = jnp.where(live, value, -jnp.inf)
        scores[row, :, span] = value
        most[row] = jnp.maximum(most[row], value) if part else value

    where_live(lambda row, part: copy(row, part).start())
    where_live(score)
    tops = [jnp.max(most[row], axis=1, keepdims=True) for row in range(rows)]

    def mix(row, part):
        span = slice(part * size, (part + 1) * size)
        shares = jnp.exp(scores[row, :, span] - tops[row])
        norm[row] = norm[row] + shares if part else shares
        value = lax.dot_general(
            shares.astype(bf16),
            held[row, :latent, span],
            (((1,), (1,)), ((), ())),
            preferred_element_type=f32,
        )
        mixed[row] = mixed[row] + value if part else value

    where_live(mix)
    lines = out.shape[0]
    line, head = iota((lines, heads), 0), iota((lines, heads), 1)
    a, b, c = line >> 6, (line >> 4) & 3, line & 3
    wanted = jnp.where(at[0] == 0, a * 16 + b * 4 + c, c * 16 + a * 4 + b)
    placed = jnp.zeros((lines, latent), f32)
    for row in range(rows):
        done = (mixed[row] / jnp.sum(norm[row], axis=1, keepdims=True)).astype(bf16)
        pick = ((wanted == head) & (((line >> 2) & 3) == row)).astype(f32).astype(bf16)
        placed = placed + jnp.dot(pick, done, preferred_element_type=f32)
    out[...] = placed.astype(bf16)


def attend(lengths, at, queries, cache):
    rows, heads, width = queries.shape
    cache_length = cache.shape[2]
    size = min(CHUNK, cache_length)
    latent = width - 64
    lines = rows * heads
    smem = pl.BlockSpec(memory_space=pltpu.SMEM)
    vmem = pl.BlockSpec(memory_space=pltpu.VMEM)
    return call(
        attend_kernel,
        jax.ShapeDtypeStruct((lines, latent), bf16),
        (lengths, at, queries, cache),
        2 * lines * cache_length * (width + latent),
        56,
        in_specs=[smem, smem, vmem, pl.BlockSpec(memory_space=pltpu.HBM)],
        out_specs=vmem,
        scratch_shapes=[
            pltpu.VMEM(cache.shape, bf16),
            pltpu.VMEM((rows, heads, cache_length), f32),
            pltpu.VMEM((rows, heads, size), f32),
            pltpu.VMEM((rows, heads, size), f32),
            pltpu.VMEM((rows, heads, latent), f32),
            pltpu.SemaphoreType.DMA((rows, cache_length // size)),
        ],
    )


def heads_kernel(at, latents, w0, w1, w2, w3, out):
    lines = latents.shape[0]
    depth, latent = w0.shape
    line = iota((lines, depth), 0)
    count = lines // SIDE
    gather = (iota((count, lines), 0) == (iota((count, lines), 1) >> 2)).astype(f32).astype(bf16)
    for step, w in enumerate((w0, w1, w2, w3)):
        head = back(at[3], step)
        value = jnp.zeros((lines, depth), f32)
        for k in range(latent // depth):
            span = slice(k * depth, (k + 1) * depth)
            value = value + jnp.dot(latents[:, span], w[:, span], preferred_element_type=f32)
        value = jnp.where((line & 3) == head, value, 0.0).astype(bf16)
        out[head] = jnp.dot(gather, value, preferred_element_type=f32).astype(bf16)


def project_kernel(at, h0, h1, h2, h3, p0, p1, p2, p3, o0, o1, o2, o3, lines):
    packs = (p0, p1, p2, p3)
    heads, _, depth = h0.shape
    block = o0.shape[1] - EXTRA
    latent = p0.shape[1] - block
    a, b, c = at[1], at[2], at[3]
    for step in range(SIDE):
        rows = pl.ds(pl.multiple_of(ahead(a, step) * GROUP, GROUP), GROUP)
        for j, h in enumerate((h0, h1, h2, h3)):
            for k in range(heads):
                lines[step, back(c, j), :, k * depth : (k + 1) * depth] = h[back(c, k), rows, :]
    for step, out in enumerate((o0, o1, o2, o3)):
        left = lines[step].reshape(SIDE * GROUP, heads * depth)
        total = jnp.zeros((SIDE * GROUP, block), f32)
        for k, pack in enumerate(packs):
            total = total + jnp.dot(
                left[:, k * depth : (k + 1) * depth],
                pack[:depth, latent:],
                preferred_element_type=f32,
            )
        out[:, :block] = total.astype(bf16)
        out[:, block:] = jnp.zeros((SIDE * GROUP, EXTRA), bf16)
    move = iota((GROUP, GROUP), 0) == b * 4 + iota((GROUP, GROUP), 1)
    move = (move & (iota((GROUP, GROUP), 1) < 4)).astype(f32).astype(bf16)
    for j, pack in enumerate(packs):
        rows = pl.ds(pl.multiple_of(back(c, j) * GROUP, GROUP), GROUP)
        own = jnp.dot(move, pack[depth:, : block + EXTRA], preferred_element_type=f32)
        o0[rows, :] = (o0[rows, :].astype(f32) + own).astype(bf16)


def norm_kernel(at, s0, s1, s2, s3, gain, out, mine):
    slots = (s0, s1, s2, s3)
    width = gain.shape[1]
    block = width // SIDE
    squares = 0.0
    for slot in slots:
        value = slot[:, :block].astype(f32)
        squares = squares + jnp.sum(value * value, axis=1, keepdims=True)
    factor = lax.rsqrt(squares * (1.0 / width) + epsilon)
    rows = pl.ds(pl.multiple_of(at[3] * GROUP, GROUP), GROUP)
    for step, slot in enumerate(slots):
        to = lanes(back(at[3], step), block)
        out[:, to] = (slot[:, :block].astype(f32) * factor * gain[:, to]).astype(bf16)
        mine[:, to] = slot[rows, :block]
    out[:, width:] = s0[:, block:]


def experts_kernel(count, parts, at, *refs):
    xs, ws, refs = refs[:count], refs[count : 2 * count], refs[2 * count :]
    gates, ups, downs, refs = refs[0:2], refs[2:4], refs[4:6], refs[6:]
    outs, (gate_sum, up_sum, hidden, weights) = refs[:-4], refs[-4:]
    step = pl.program_id(0)
    units = gates[0].shape[2]
    rows = outs[0].shape[0]

    def joined(refs):
        return refs[0][...] if count == 1 else jnp.concatenate([r[...] for r in refs], axis=0)

    @pl.when(step < parts)
    def _():
        x = joined(xs)
        for k in range(2):
            span = slice(k * units, (k + 1) * units)
            gate = jnp.dot(x, gates[k][0], preferred_element_type=f32)
            up = jnp.dot(x, ups[k][0], preferred_element_type=f32)

            @pl.when(step == 0)
            def _():
                gate_sum[:, span] = gate
                up_sum[:, span] = up

            @pl.when(step > 0)
            def _():
                gate_sum[:, span] += gate
                up_sum[:, span] += up

    @pl.when(step == parts - 1)
    def _():
        gate = gate_sum[...]
        hidden[...] = (gate * (1.0 / (1.0 + jnp.exp(-gate))) * up_sum[...]).astype(bf16)
        told = joined(ws).astype(f32)
        for k in range(2):
            chosen = iota(told.shape, 1) == at[4 + k]
            weight = jnp.sum(jnp.where(chosen, told, 0.0), axis=1, keepdims=True)
            weights[k] = jnp.broadcast_to(weight, told.shape)

    @pl.when(step >= parts)
    def _():
        total = 0.0
        for k in range(2):
            value = jnp.dot(
                hidden[:, k * units : (k + 1) * units], downs[k][0], preferred_element_type=f32
            )
            total = total + value * weights[k][:, 0:1]
        for k, out in enumerate(outs):
            out[...] = total[k * rows : (k + 1) * rows].astype(bf16)


def experts(at, slots, gates, ups, downs, pieces):
    count, parts = len(slots), 2
    rows = slots[0].shape[0]
    width, units = gates[0].shape[1:]
    block = width // parts

    def first(i):
        return jnp.minimum(i, parts - 1)

    def second(i):
        return jnp.maximum(i - parts, 0)

    in_specs = [pl.BlockSpec(memory_space=pltpu.SMEM)]
    in_specs += [pl.BlockSpec((rows, block), lambda i: (0, first(i)))] * count
    in_specs += [pl.BlockSpec((rows, EXTRA), lambda i: (0, width // EXTRA))] * count
    in_specs += [pl.BlockSpec((1, block, units), lambda i: (0, first(i), 0))] * 4
    in_specs += [pl.BlockSpec((1, units, block), lambda i: (0, 0, second(i)))] * 2
    return call(
        functools.partial(experts_kernel, count, parts),
        [jax.ShapeDtypeStruct((count * rows // pieces, width), bf16)] * pieces,
        (at, *slots, *slots, *gates, *ups, *downs),
        12 * count * rows * width * units,
        28,
        grid=(2 * parts,),
        in_specs=in_specs,
        out_specs=[pl.BlockSpec((count * rows // pieces, block), lambda i: (0, second(i)))]
        * pieces,
        scratch_shapes=[
            pltpu.VMEM((count * rows, 2 * units), f32),
            pltpu.VMEM((count * rows, 2 * units), f32),
            pltpu.VMEM((count * rows, 2 * units), bf16),
            pltpu.VMEM((2, count * rows, EXTRA), f32),
        ],
    )


def load_kernel(at, x, *refs):
    sources, out, held, refs = refs[:6], refs[6], refs[7:13], refs[13:]
    gate_sum, up_sum, hidden, sems = refs
    gates, ups, downs = held[0:2], held[2:4], held[4:6]
    _, width, units = gates[0].shape
    step = width // SIDE

    def copy(k, i):
        span = pl.ds(i * step, step)
        where = (0, span) if k < 4 else (0, slice(None), span)
        return pltpu.make_async_copy(sources[k].at[where], held[k].at[where], sems.at[k, i])

    for i in range(SIDE):
        for k in range(4):
            copy(k, i).start()
    for i in range(SIDE):
        for k in (4, 5):
            copy(k, i).start()
    for i in range(SIDE):
        span = slice(i * step, (i + 1) * step)
        for k in range(4):
            copy(k, i).wait()
        for k in range(2):
            to = slice(k * units, (k + 1) * units)
            gate = jnp.dot(x[:, span], gates[k][0, span, :], preferred_element_type=f32)
            up = jnp.dot(x[:, span], ups[k][0, span, :], preferred_element_type=f32)
            gate_sum[:, to] = gate_sum[:, to] + gate if i else gate
            up_sum[:, to] = up_sum[:, to] + up if i else up
    gate = gate_sum[...]
    hidden[...] = (gate * (1.0 / (1.0 + jnp.exp(-gate))) * up_sum[...]).astype(bf16)
    told = x[:, width:].astype(f32)
    weights = []
    for k in range(2):
        chosen = iota(told.shape, 1) == at[4 + k]
        weights.append(jnp.sum(jnp.where(chosen, told, 0.0), axis=1, keepdims=True))
    for i in range(SIDE):
        span = slice(i * step, (i + 1) * step)
        total = 0.0
        for k in range(2):
            copy(4 + k, i).wait()
            left = hidden[:, k * units : (k + 1) * units]
            value = jnp.dot(left, downs[k][0, :, span], preferred_element_type=f32)
            total = total + value * weights[k]
        out[:, span] = total.astype(bf16)


def experts_and_load(at, x, gates, ups, downs):
    rows = x.shape[0]
    width, units = gates[0].shape[1:]
    blocks = (*gates, *ups, *downs)
    smem, vmem = [pl.BlockSpec(memory_space=m) for m in (pltpu.SMEM, pltpu.VMEM)]
    out, *held = call(
        load_kernel,
        [jax.ShapeDtypeStruct((rows, width), bf16)]
        + [jax.ShapeDtypeStruct(v.shape, bf16) for v in blocks],
        (at, x, *blocks),
        12 * rows * width * units,
        30,
        in_specs=[smem, vmem] + [pl.BlockSpec(memory_space=pltpu.HBM)] * 6,
        out_specs=[vmem] * 7,
        scratch_shapes=[
            pltpu.VMEM((rows, 2 * units), f32),
            pltpu.VMEM((rows, 2 * units), f32),
            pltpu.VMEM((rows, 2 * units), bf16),
            pltpu.SemaphoreType.DMA((6, SIDE)),
        ],
    )
    return out, held[0:2], held[2:4], held[4:6]


def on_device(
    queries,
    latent_cache,
    lengths,
    residual,
    w_uv,
    w_out,
    norm_gain,
    expert_ids,
    gate_values,
    w_gate,
    w_up,
    w_down,
):
    role, dev = lax.axis_index("role"), lax.axis_index("dev")
    x, y, z = dev // 16, dev // 4 % 4, dev % 4
    first = role == 0
    a, b, c = jnp.where(first, x, y), jnp.where(first, y, z), jnp.where(first, z, x)
    per_expert = 128 // EXPERTS
    experts_here = [(role * 64 + dev) // per_expert, ((1 - role) * 64 + dev) // per_expert]
    at = jnp.stack([role, a, b, c, *experts_here, role, role]).astype(jnp.int32)
    rows, width = residual.shape
    latent, depth = w_uv.shape[1:]
    block = width // SIDE
    count = GROUP * SIDE

    shape = jax.ShapeDtypeStruct((depth + GROUP, latent + block), bf16)
    packs = call(
        bundle_kernel,
        [shape] * SIDE,
        (at, w_out, w_uv, residual, expert_ids, gate_values),
        0,
        60,
        grid=(1,),
        in_specs=[pl.BlockSpec(memory_space=pltpu.SMEM)]
        + [
            pl.BlockSpec(v.shape, lambda i, n=v.ndim: (0,) * n)
            for v in (w_out, w_uv, residual, expert_ids, gate_values)
        ],
        out_specs=[pl.BlockSpec(shape.shape, lambda i: (0, 0))] * SIDE,
    )
    packs = [packs[0]] + [shift(packs[s], "c", s) for s in (1, 2, 3)]
    gates, ups, downs = [(w, swap_cores(w)) for w in (w_gate, w_up, w_down)]

    sent = attend(lengths, at, queries, latent_cache.swapaxes(1, 2)).reshape(16, SIDE * rows, latent)
    got = lax.all_to_all(sent, AXES, 0, 0, axis_index_groups=groups("ab"), tiled=True)
    got, gates, ups, downs = lax.optimization_barrier((got, gates, ups, downs))
    got = got.reshape(-1, latent)
    vmem = pl.BlockSpec(memory_space=pltpu.VMEM)
    head_out = call(
        heads_kernel,
        jax.ShapeDtypeStruct((SIDE, count, depth), bf16),
        (at, got, *packs),
        2 * SIDE * got.size * depth,
        16,
        grid=(1,),
        in_specs=[pl.BlockSpec(memory_space=pltpu.SMEM), vmem]
        + [pl.BlockSpec((depth, latent), lambda i: (0, 0))] * SIDE,
        out_specs=vmem,
    )
    gathered = shifts(head_out, "c")
    partial = call(
        project_kernel,
        [jax.ShapeDtypeStruct((count, block + EXTRA), bf16)] * SIDE,
        (at, *gathered, *packs),
        2 * SIDE * count * SIDE * depth * block,
        24,
        scratch_shapes=[pltpu.VMEM((SIDE, SIDE, GROUP, SIDE * depth), bf16)],
    )

    def added(parts):
        return functools.reduce(lambda u, v: u + v, [p.astype(f32) for p in parts]).astype(bf16)

    total = added([partial[0]] + [shift(partial[s], "a", s) for s in (2, 1, 3)])
    attended = added(shifts(total, "b"))
    columns = shifts(attended, "c")
    normed, mine = call(
        norm_kernel,
        [
            jax.ShapeDtypeStruct((count, width + EXTRA), bf16),
            jax.ShapeDtypeStruct((GROUP, width), bf16),
        ],
        (at, *columns, norm_gain.astype(f32).reshape(1, width)),
        0,
        16,
    )

    own_sum, gates, ups, downs = experts_and_load(at, normed, gates, ups, downs)
    near = [shift(normed, "a", s) for s in (1, 3)]
    near, own_sum = lax.optimization_barrier((near, own_sum))
    half = count // 2
    far = [shift(near[0][:half], "a", 1), shift(near[1][half:], "a", 3)]
    near_sums = experts(at, near, gates, ups, downs, 2)
    (far_sum,) = experts(at, far, gates, ups, downs, 1)
    sums = [shift(near_sums[0], "a", -1), shift(near_sums[1], "a", -3), shift(far_sum, "a", -2)]
    last = added([own_sum] + sums).reshape(16, rows, width)
    last = lax.all_to_all(last, AXES, 0, 0, axis_index_groups=groups("cb"), tiled=True)
    combined = jnp.sum(last.astype(f32), axis=0)
    mine = lax.dynamic_slice_in_dim(mine, b * rows, rows, 0)
    return (mine.astype(f32) + combined).astype(bf16)


def solution(mesh):
    return jax.shard_map(
        on_device,
        mesh=mesh,
        in_specs=(
            P(("role", "dev"), None, None),
            P(("role", "dev"), None, None),
            P(("role", "dev")),
            P(("role", "dev"), None),
            P("dev", None, None),
            P("dev", None),
            P(),
            P(("role", "dev"), None),
            P(("role", "dev"), None),
            P(("role", "dev"), None, None),
            P(("role", "dev"), None, None),
            P(("role", "dev"), None, None),
        ),
        out_specs=P(("role", "dev"), None),
        check_vma=False,
    )
```

```python
import functools
import itertools

import jax
import jax.numpy as jnp
from jax import lax
from jax.experimental import pallas as pl
from jax.experimental.pallas import tpu as pltpu
from jax.sharding import PartitionSpec as P

EXPERTS = 16
AXES = ("role", "dev")
SIDE = 4
EXTRA = 128
GROUP = 16
CHUNK = 1024

score_scale = 192.0 ** (-0.5)
epsilon = 1e-06
bf16, f32 = jnp.bfloat16, jnp.float32


ORDERS = ("xzy", "zyx")
PLACE = {"x": 16, "y": 4, "z": 1}


def device_at(role, a, b, c):
    return role * 64 + sum(PLACE[axis] * at for axis, at in zip(ORDERS[role], (a, b, c)))


def groups(along):
    rest = [axis for axis in "abc" if axis not in along]
    out = []
    for role in range(2):
        for fixed in itertools.product(range(SIDE), repeat=len(rest)):
            group = []
            for moving in itertools.product(range(SIDE), repeat=len(along)):
                at = dict(zip(rest, fixed))
                at.update(zip(along, moving))
                group.append(device_at(role, at["a"], at["b"], at["c"]))
            out.append(group)
    return out


def shift(value, axis, step):
    pairs = []
    for group in groups(axis):
        pairs += [(group[i], group[(i + step) % SIDE]) for i in range(SIDE)]
    return lax.ppermute(value, AXES, pairs)


def shifts(value, axis):
    got = {step: shift(value, axis, step) for step in (2, 1, 3)}
    return [value] + [got[step] for step in (1, 2, 3)]


def swap_cores(value):
    return lax.ppermute(value, "role", [(0, 1), (1, 0)])


def call(body, out_shape, args, flops, limit, **given):
    smem = pl.BlockSpec(memory_space=pltpu.SMEM)
    vmem = pl.BlockSpec(memory_space=pltpu.VMEM)
    if "in_specs" not in given:
        given["in_specs"] = [smem] + [vmem] * (len(args) - 1)
        given["out_specs"] = jax.tree.map(lambda _: vmem, out_shape)
    moved = sum(x.size * x.dtype.itemsize for x in [*args, *jax.tree.leaves(out_shape)])
    return pl.pallas_call(
        body,
        out_shape=out_shape,
        compiler_params=pltpu.CompilerParams(vmem_limit_bytes=limit * 2**20),
        cost_estimate=pl.CostEstimate(
            flops=flops, bytes_accessed=moved if flops else 0, transcendentals=0
        ),
        **given,
    )(*args)


def back(mine, step):
    return lax.rem(mine - step + SIDE, SIDE)


def ahead(mine, step):
    return lax.rem(mine + step, SIDE)


def lanes(at, width):
    return pl.ds(pl.multiple_of(at * width, width), width)


def iota(shape, axis):
    return lax.broadcasted_iota(jnp.int32, shape, axis)


def bundle_kernel(at, w_out, w_uv, residual, ids, gates, *outs):
    c = at[3]
    latent, depth = w_uv.shape[1], w_out.shape[0]
    rows, width = residual.shape
    block = width // SIDE
    weights = jnp.zeros((rows, EXTRA), f32)
    for k in range(ids.shape[1]):
        named = ids[:, k : k + 1] == iota((rows, EXTRA), 1)
        weights = weights + jnp.where(named, gates[:, k : k + 1].astype(f32), 0.0)
    spread = (iota((GROUP, rows), 0) == iota((GROUP, rows), 1)).astype(f32).astype(bf16)

    def place(value):
        return jnp.dot(spread, value, preferred_element_type=f32).astype(bf16)

    weights = place(weights.astype(bf16))
    for step, out in enumerate(outs):
        to = lanes(ahead(c, step), block)
        for k in range(latent // depth):
            out[:depth, k * depth : (k + 1) * depth] = w_uv[0, k * depth : (k + 1) * depth, :]
        out[:depth, latent:] = w_out[:, to]
        out[depth:, :block] = place(residual[:, to])
        out[depth:, block : block + EXTRA] = weights
        if latent > EXTRA:
            out[depth:, block + EXTRA :] = jnp.zeros((GROUP, latent - EXTRA), bf16)


def attend_kernel(lengths, at, query, cache, out, held, scores, most, norm, mixed, done, sems):
    rows, heads, _ = query.shape
    latent = mixed.shape[2]
    size = most.shape[2]
    parts = cache.shape[2] // size

    def copy(row, part):
        span = pl.ds(part * size, size)
        return pltpu.make_async_copy(
            cache.at[row, :, span], held.at[row, :, span], sems.at[row, part]
        )

    def where_live(step):
        for row in range(rows):
            for part in range(parts):
                act = functools.partial(step, row, part)
                if part:
                    pl.when(part * size < lengths[row])(act)
                else:
                    act()

    def score(row, part):
        span = slice(part * size, (part + 1) * size)
        copy(row, part).wait()
        value = score_scale * jnp.dot(query[row], held[row, :, span], preferred_element_type=f32)
        live = part * size + iota(value.shape, 1) < lengths[row]
        value = jnp.where(live, value, -jnp.inf)
        scores[row, :, span] = value
        most[row] = jnp.maximum(most[row], value) if part else value

    where_live(lambda row, part: copy(row, part).start())
    where_live(score)
    tops = [jnp.max(most[row], axis=1, keepdims=True) for row in range(rows)]

    def mix(row, part):
        span = slice(part * size, (part + 1) * size)
        shares = jnp.exp(scores[row, :, span] - tops[row])
        norm[row] = norm[row] + shares if part else shares
        value = lax.dot_general(
            shares.astype(bf16),
            held[row, :latent, span],
            (((1,), (1,)), ((), ())),
            preferred_element_type=f32,
        )
        mixed[row] = mixed[row] + value if part else value

    where_live(mix)
    lines = out.shape[0]
    line = iota((lines, rows * heads), 0)
    a, b, c = line >> 6, (line >> 4) & 3, line & 3
    orders = [sum(PLACE[axis] * v for axis, v in zip(order, (a, b, c))) for order in ORDERS]
    wanted = jnp.where(at[0] == 0, *orders) + heads * ((line >> 2) & 3)
    pick = (wanted == iota((lines, rows * heads), 1)).astype(f32).astype(bf16)
    for row in range(rows):
        value = mixed[row] / jnp.sum(norm[row], axis=1, keepdims=True)
        done[row * heads : (row + 1) * heads, :] = value.astype(bf16)
    out[...] = jnp.dot(pick, done[...], preferred_element_type=f32).astype(bf16)


def attend(lengths, at, queries, cache):
    rows, heads, width = queries.shape
    cache_length = cache.shape[2]
    size = min(CHUNK, cache_length)
    latent = width - 64
    lines = rows * heads
    smem = pl.BlockSpec(memory_space=pltpu.SMEM)
    vmem = pl.BlockSpec(memory_space=pltpu.VMEM)
    return call(
        attend_kernel,
        jax.ShapeDtypeStruct((lines, latent), bf16),
        (lengths, at, queries, cache),
        2 * lines * cache_length * (width + latent),
        56,
        in_specs=[smem, smem, vmem, pl.BlockSpec(memory_space=pltpu.HBM)],
        out_specs=vmem,
        scratch_shapes=[
            pltpu.VMEM(cache.shape, bf16),
            pltpu.VMEM((rows, heads, cache_length), f32),
            pltpu.VMEM((rows, heads, size), f32),
            pltpu.VMEM((rows, heads, size), f32),
            pltpu.VMEM((rows, heads, latent), f32),
            pltpu.VMEM((lines, latent), bf16),
            pltpu.SemaphoreType.DMA((rows, cache_length // size)),
        ],
    )


def heads_kernel(at, latents, w0, w1, w2, w3, out):
    lines = latents.shape[0]
    depth, latent = w0.shape
    line = iota((lines, depth), 0)
    count = lines // SIDE
    gather = (iota((count, lines), 0) == (iota((count, lines), 1) >> 2)).astype(f32).astype(bf16)
    for step, w in enumerate((w0, w1, w2, w3)):
        head = back(at[3], step)
        value = jnp.zeros((lines, depth), f32)
        for k in range(latent // depth):
            span = slice(k * depth, (k + 1) * depth)
            value = value + jnp.dot(latents[:, span], w[:, span], preferred_element_type=f32)
        value = jnp.where((line & 3) == head, value, 0.0).astype(bf16)
        out[head] = jnp.dot(gather, value, preferred_element_type=f32).astype(bf16)


def project_kernel(at, h0, h1, h2, h3, p0, p1, p2, p3, o0, o1, o2, o3, lines):
    packs = (p0, p1, p2, p3)
    heads, _, depth = h0.shape
    block = o0.shape[1] - EXTRA
    latent = p0.shape[1] - block
    a, b, c = at[1], at[2], at[3]
    for step in range(SIDE):
        rows = pl.ds(pl.multiple_of(ahead(a, step) * GROUP, GROUP), GROUP)
        for j, h in enumerate((h0, h1, h2, h3)):
            for k in range(heads):
                lines[step, back(c, j), :, k * depth : (k + 1) * depth] = h[back(c, k), rows, :]
    for step, out in enumerate((o0, o1, o2, o3)):
        left = lines[step].reshape(SIDE * GROUP, heads * depth)
        total = jnp.zeros((SIDE * GROUP, block), f32)
        for k, pack in enumerate(packs):
            total = total + jnp.dot(
                left[:, k * depth : (k + 1) * depth],
                pack[:depth, latent:],
                preferred_element_type=f32,
            )
        out[:, :block] = total.astype(bf16)
        out[:, block:] = jnp.zeros((SIDE * GROUP, EXTRA), bf16)
    move = iota((GROUP, GROUP), 0) == b * 4 + iota((GROUP, GROUP), 1)
    move = (move & (iota((GROUP, GROUP), 1) < 4)).astype(f32).astype(bf16)
    for j, pack in enumerate(packs):
        rows = pl.ds(pl.multiple_of(back(c, j) * GROUP, GROUP), GROUP)
        own = jnp.dot(move, pack[depth:, : block + EXTRA], preferred_element_type=f32)
        o0[rows, :] = (o0[rows, :].astype(f32) + own).astype(bf16)


def norm_kernel(at, s0, s1, s2, s3, gain, out, mine):
    slots = (s0, s1, s2, s3)
    width = gain.shape[1]
    block = width // SIDE
    squares = 0.0
    for slot in slots:
        value = slot[:, :block].astype(f32)
        squares = squares + jnp.sum(value * value, axis=1, keepdims=True)
    factor = lax.rsqrt(squares * (1.0 / width) + epsilon)
    rows = pl.ds(pl.multiple_of(at[3] * GROUP, GROUP), GROUP)
    for step, slot in enumerate(slots):
        to = lanes(back(at[3], step), block)
        out[:, to] = (slot[:, :block].astype(f32) * factor * gain[:, to]).astype(bf16)
        mine[:, to] = slot[rows, :block]
    out[:, width:] = s0[:, block:]


def experts_kernel(count, parts, at, *refs):
    xs, ws, refs = refs[:count], refs[count : 2 * count], refs[2 * count :]
    gates, ups, downs, refs = refs[0:2], refs[2:4], refs[4:6], refs[6:]
    outs, (gate_sum, up_sum, hidden, weights) = refs[:-4], refs[-4:]
    step = pl.program_id(0)
    units = gates[0].shape[2]
    rows = outs[0].shape[0]

    def joined(refs):
        return refs[0][...] if count == 1 else jnp.concatenate([r[...] for r in refs], axis=0)

    @pl.when(step < parts)
    def _():
        x = joined(xs)
        for k in range(2):
            span = slice(k * units, (k + 1) * units)
            gate = jnp.dot(x, gates[k][0], preferred_element_type=f32)
            up = jnp.dot(x, ups[k][0], preferred_element_type=f32)

            @pl.when(step == 0)
            def _():
                gate_sum[:, span] = gate
                up_sum[:, span] = up

            @pl.when(step > 0)
            def _():
                gate_sum[:, span] += gate
                up_sum[:, span] += up

    @pl.when(step == parts - 1)
    def _():
        gate = gate_sum[...]
        hidden[...] = (gate * (1.0 / (1.0 + jnp.exp(-gate))) * up_sum[...]).astype(bf16)
        told = joined(ws).astype(f32)
        for k in range(2):
            chosen = iota(told.shape, 1) == at[4 + k]
            weight = jnp.sum(jnp.where(chosen, told, 0.0), axis=1, keepdims=True)
            weights[k] = jnp.broadcast_to(weight, told.shape)

    @pl.when(step >= parts)
    def _():
        total = 0.0
        for k in range(2):
            value = jnp.dot(
                hidden[:, k * units : (k + 1) * units], downs[k][0], preferred_element_type=f32
            )
            total = total + value * weights[k][:, 0:1]
        for k, out in enumerate(outs):
            out[...] = total[k * rows : (k + 1) * rows].astype(bf16)


def experts(at, slots, gates, ups, downs, pieces):
    count, parts = len(slots), 2
    rows = slots[0].shape[0]
    width, units = gates[0].shape[1:]
    block = width // parts

    def first(i):
        return jnp.minimum(i, parts - 1)

    def second(i):
        return jnp.maximum(i - parts, 0)

    in_specs = [pl.BlockSpec(memory_space=pltpu.SMEM)]
    in_specs += [pl.BlockSpec((rows, block), lambda i: (0, first(i)))] * count
    in_specs += [pl.BlockSpec((rows, EXTRA), lambda i: (0, width // EXTRA))] * count
    in_specs += [pl.BlockSpec((1, block, units), lambda i: (0, first(i), 0))] * 4
    in_specs += [pl.BlockSpec((1, units, block), lambda i: (0, 0, second(i)))] * 2
    return call(
        functools.partial(experts_kernel, count, parts),
        [jax.ShapeDtypeStruct((count * rows // pieces, width), bf16)] * pieces,
        (at, *slots, *slots, *gates, *ups, *downs),
        12 * count * rows * width * units,
        28,
        grid=(2 * parts,),
        in_specs=in_specs,
        out_specs=[pl.BlockSpec((count * rows // pieces, block), lambda i: (0, second(i)))]
        * pieces,
        scratch_shapes=[
            pltpu.VMEM((count * rows, 2 * units), f32),
            pltpu.VMEM((count * rows, 2 * units), f32),
            pltpu.VMEM((count * rows, 2 * units), bf16),
            pltpu.VMEM((2, count * rows, EXTRA), f32),
        ],
    )


def load_kernel(at, x, *refs):
    sources, out, held, refs = refs[:6], refs[6], refs[7:13], refs[13:]
    gate_sum, up_sum, hidden, sems = refs
    gates, ups, downs = held[0:2], held[2:4], held[4:6]
    _, width, units = gates[0].shape
    step = width // SIDE

    def copy(k, i):
        span = pl.ds(i * step, step)
        where = (0, span) if k < 4 else (0, slice(None), span)
        return pltpu.make_async_copy(sources[k].at[where], held[k].at[where], sems.at[k, i])

    for i in range(SIDE):
        for k in range(4):
            copy(k, i).start()
    for i in range(SIDE):
        for k in (4, 5):
            copy(k, i).start()
    for i in range(SIDE):
        span = slice(i * step, (i + 1) * step)
        for k in range(4):
            copy(k, i).wait()
        for k in range(2):
            to = slice(k * units, (k + 1) * units)
            gate = jnp.dot(x[:, span], gates[k][0, span, :], preferred_element_type=f32)
            up = jnp.dot(x[:, span], ups[k][0, span, :], preferred_element_type=f32)
            gate_sum[:, to] = gate_sum[:, to] + gate if i else gate
            up_sum[:, to] = up_sum[:, to] + up if i else up
    gate = gate_sum[...]
    hidden[...] = (gate * (1.0 / (1.0 + jnp.exp(-gate))) * up_sum[...]).astype(bf16)
    told = x[:, width:].astype(f32)
    weights = []
    for k in range(2):
        chosen = iota(told.shape, 1) == at[4 + k]
        weights.append(jnp.sum(jnp.where(chosen, told, 0.0), axis=1, keepdims=True))
    for i in range(SIDE):
        span = slice(i * step, (i + 1) * step)
        total = 0.0
        for k in range(2):
            copy(4 + k, i).wait()
            left = hidden[:, k * units : (k + 1) * units]
            value = jnp.dot(left, downs[k][0, :, span], preferred_element_type=f32)
            total = total + value * weights[k]
        out[:, span] = total.astype(bf16)


def experts_and_load(at, x, gates, ups, downs):
    rows = x.shape[0]
    width, units = gates[0].shape[1:]
    blocks = (*gates, *ups, *downs)
    smem, vmem = [pl.BlockSpec(memory_space=m) for m in (pltpu.SMEM, pltpu.VMEM)]
    out, *held = call(
        load_kernel,
        [jax.ShapeDtypeStruct((rows, width), bf16)]
        + [jax.ShapeDtypeStruct(v.shape, bf16) for v in blocks],
        (at, x, *blocks),
        12 * rows * width * units,
        30,
        in_specs=[smem, vmem] + [pl.BlockSpec(memory_space=pltpu.HBM)] * 6,
        out_specs=[vmem] * 7,
        scratch_shapes=[
            pltpu.VMEM((rows, 2 * units), f32),
            pltpu.VMEM((rows, 2 * units), f32),
            pltpu.VMEM((rows, 2 * units), bf16),
            pltpu.SemaphoreType.DMA((6, SIDE)),
        ],
    )
    return out, held[0:2], held[2:4], held[4:6]


def on_device(
    queries,
    latent_cache,
    lengths,
    residual,
    w_uv,
    w_out,
    norm_gain,
    expert_ids,
    gate_values,
    w_gate,
    w_up,
    w_down,
):
    role, dev = lax.axis_index("role"), lax.axis_index("dev")
    a, b, c = [
        jnp.where(role == 0, *[dev // PLACE[order[i]] % SIDE for order in ORDERS]) for i in range(3)
    ]
    per_expert = 128 // EXPERTS
    experts_here = [(role * 64 + dev) // per_expert, ((1 - role) * 64 + dev) // per_expert]
    at = jnp.stack([role, a, b, c, *experts_here, role, role]).astype(jnp.int32)
    rows, width = residual.shape
    latent, depth = w_uv.shape[1:]
    block = width // SIDE
    count = GROUP * SIDE

    shape = jax.ShapeDtypeStruct((depth + GROUP, latent + block), bf16)
    packs = call(
        bundle_kernel,
        [shape] * SIDE,
        (at, w_out, w_uv, residual, expert_ids, gate_values),
        0,
        60,
        grid=(1,),
        in_specs=[pl.BlockSpec(memory_space=pltpu.SMEM)]
        + [
            pl.BlockSpec(v.shape, lambda i, n=v.ndim: (0,) * n)
            for v in (w_out, w_uv, residual, expert_ids, gate_values)
        ],
        out_specs=[pl.BlockSpec(shape.shape, lambda i: (0, 0))] * SIDE,
    )
    packs = [packs[0]] + [shift(packs[s], "c", s) for s in (1, 2, 3)]
    gates, ups, downs = [(w, swap_cores(w)) for w in (w_gate, w_up, w_down)]

    sent = attend(lengths, at, queries, latent_cache.swapaxes(1, 2)).reshape(16, SIDE * rows, latent)
    got = lax.all_to_all(sent, AXES, 0, 0, axis_index_groups=groups("ab"), tiled=True)
    got, gates, ups, downs = lax.optimization_barrier((got, gates, ups, downs))
    got = got.reshape(-1, latent)
    vmem = pl.BlockSpec(memory_space=pltpu.VMEM)
    head_out = call(
        heads_kernel,
        jax.ShapeDtypeStruct((SIDE, count, depth), bf16),
        (at, got, *packs),
        2 * SIDE * got.size * depth,
        16,
        grid=(1,),
        in_specs=[pl.BlockSpec(memory_space=pltpu.SMEM), vmem]
        + [pl.BlockSpec((depth, latent), lambda i: (0, 0))] * SIDE,
        out_specs=vmem,
    )
    gathered = shifts(head_out, "c")
    partial = call(
        project_kernel,
        [jax.ShapeDtypeStruct((count, block + EXTRA), bf16)] * SIDE,
        (at, *gathered, *packs),
        2 * SIDE * count * SIDE * depth * block,
        24,
        scratch_shapes=[pltpu.VMEM((SIDE, SIDE, GROUP, SIDE * depth), bf16)],
    )

    def added(parts):
        return functools.reduce(lambda u, v: u + v, [p.astype(f32) for p in parts]).astype(bf16)

    total = added([partial[0]] + [shift(partial[s], "a", s) for s in (2, 1, 3)])
    attended = added(shifts(total, "b"))
    columns = shifts(attended, "c")
    normed, mine = call(
        norm_kernel,
        [
            jax.ShapeDtypeStruct((count, width + EXTRA), bf16),
            jax.ShapeDtypeStruct((GROUP, width), bf16),
        ],
        (at, *columns, norm_gain.astype(f32).reshape(1, width)),
        0,
        16,
    )

    own_sum, gates, ups, downs = experts_and_load(at, normed, gates, ups, downs)
    near = [shift(normed, "a", s) for s in (1, 3)]
    near, own_sum = lax.optimization_barrier((near, own_sum))
    half = count // 2
    far = [shift(near[0][:half], "a", 1), shift(near[1][half:], "a", 3)]
    near_sums = experts(at, near, gates, ups, downs, 2)
    (far_sum,) = experts(at, far, gates, ups, downs, 1)
    sums = [shift(near_sums[0], "a", -1), shift(near_sums[1], "a", -3), shift(far_sum, "a", -2)]
    last = added([own_sum] + sums).reshape(16, rows, width)
    last = lax.all_to_all(last, AXES, 0, 0, axis_index_groups=groups("cb"), tiled=True)
    combined = jnp.sum(last.astype(f32), axis=0)
    mine = lax.dynamic_slice_in_dim(mine, b * rows, rows, 0)
    return (mine.astype(f32) + combined).astype(bf16)


def solution(mesh):
    return jax.shard_map(
        on_device,
        mesh=mesh,
        in_specs=(
            P(("role", "dev"), None, None),
            P(("role", "dev"), None, None),
            P(("role", "dev")),
            P(("role", "dev"), None),
            P("dev", None, None),
            P("dev", None),
            P(),
            P(("role", "dev"), None),
            P(("role", "dev"), None),
            P(("role", "dev"), None, None),
            P(("role", "dev"), None, None),
            P(("role", "dev"), None, None),
        ),
        out_specs=P(("role", "dev"), None),
        check_vma=False,
    )
```

```python
import functools
import itertools

import jax
import jax.numpy as jnp
from jax import lax
from jax.experimental import pallas as pl
from jax.experimental.pallas import tpu as pltpu
from jax.sharding import PartitionSpec as P

EXPERTS = 16
AXES = ("role", "dev")
SIDE = 4
EXTRA = 128
GROUP = 16
CHUNK = 1024

score_scale = 192.0 ** (-0.5)
epsilon = 1e-06
bf16, f32 = jnp.bfloat16, jnp.float32


ORDERS = ("xzy", "zyx")
PLACE = {"x": 16, "y": 4, "z": 1}


def device_at(role, a, b, c):
    return role * 64 + sum(PLACE[axis] * at for axis, at in zip(ORDERS[role], (a, b, c)))


def groups(along):
    rest = [axis for axis in "abc" if axis not in along]
    out = []
    for role in range(2):
        for fixed in itertools.product(range(SIDE), repeat=len(rest)):
            group = []
            for moving in itertools.product(range(SIDE), repeat=len(along)):
                at = dict(zip(rest, fixed))
                at.update(zip(along, moving))
                group.append(device_at(role, at["a"], at["b"], at["c"]))
            out.append(group)
    return out


def shift(value, axis, step):
    pairs = []
    for group in groups(axis):
        pairs += [(group[i], group[(i + step) % SIDE]) for i in range(SIDE)]
    return lax.ppermute(value, AXES, pairs)


def shifts(value, axis):
    got = {step: shift(value, axis, step) for step in (2, 1, 3)}
    return [value] + [got[step] for step in (1, 2, 3)]


def swap_cores(value):
    return lax.ppermute(value, "role", [(0, 1), (1, 0)])


def call(body, out_shape, args, flops, limit, **given):
    smem = pl.BlockSpec(memory_space=pltpu.SMEM)
    vmem = pl.BlockSpec(memory_space=pltpu.VMEM)
    if "in_specs" not in given:
        given["in_specs"] = [smem] + [vmem] * (len(args) - 1)
        given["out_specs"] = jax.tree.map(lambda _: vmem, out_shape)
    moved = sum(x.size * x.dtype.itemsize for x in [*args, *jax.tree.leaves(out_shape)])
    return pl.pallas_call(
        body,
        out_shape=out_shape,
        compiler_params=pltpu.CompilerParams(vmem_limit_bytes=limit * 2**20),
        cost_estimate=pl.CostEstimate(
            flops=flops, bytes_accessed=moved if flops else 0, transcendentals=0
        ),
        **given,
    )(*args)


def back(mine, step):
    return lax.rem(mine - step + SIDE, SIDE)


def ahead(mine, step):
    return lax.rem(mine + step, SIDE)


def lanes(at, width):
    return pl.ds(pl.multiple_of(at * width, width), width)


def iota(shape, axis):
    return lax.broadcasted_iota(jnp.int32, shape, axis)


def bundle_kernel(at, w_out, w_uv, residual, ids, gates, *outs):
    c = at[3]
    latent, depth = w_uv.shape[1], w_out.shape[0]
    rows, width = residual.shape
    block = width // SIDE
    weights = jnp.zeros((rows, EXTRA), f32)
    for k in range(ids.shape[1]):
        named = ids[:, k : k + 1] == iota((rows, EXTRA), 1)
        weights = weights + jnp.where(named, gates[:, k : k + 1].astype(f32), 0.0)
    spread = (iota((GROUP, rows), 0) == iota((GROUP, rows), 1)).astype(f32).astype(bf16)

    def place(value):
        return jnp.dot(spread, value, preferred_element_type=f32).astype(bf16)

    weights = place(weights.astype(bf16))
    for step, out in enumerate(outs):
        to = lanes(ahead(c, step), block)
        for k in range(latent // depth):
            out[:depth, k * depth : (k + 1) * depth] = w_uv[0, k * depth : (k + 1) * depth, :]
        out[:depth, latent:] = w_out[:, to]
        out[depth:, :block] = place(residual[:, to])
        out[depth:, block : block + EXTRA] = weights
        if latent > EXTRA:
            out[depth:, block + EXTRA :] = jnp.zeros((GROUP, latent - EXTRA), bf16)


def attend_kernel(lengths, at, query, cache, out, held, scores, most, norm, mixed, done, sems):
    rows, heads, _ = query.shape
    latent = mixed.shape[2]
    size = most.shape[2]
    parts = cache.shape[2] // size

    def copy(row, part):
        span = pl.ds(part * size, size)
        return pltpu.make_async_copy(
            cache.at[row, :, span], held.at[row, :, span], sems.at[row, part]
        )

    def where_live(step):
        for row in range(rows):
            for part in range(parts):
                act = functools.partial(step, row, part)
                if part:
                    pl.when(part * size < lengths[row])(act)
                else:
                    act()

    def score(row, part):
        span = slice(part * size, (part + 1) * size)
        copy(row, part).wait()
        value = score_scale * jnp.dot(query[row], held[row, :, span], preferred_element_type=f32)
        live = part * size + iota(value.shape, 1) < lengths[row]
        value = jnp.where(live, value, -jnp.inf)
        scores[row, :, span] = value
        most[row] = jnp.maximum(most[row], value) if part else value

    where_live(lambda row, part: copy(row, part).start())
    where_live(score)
    tops = [jnp.max(most[row], axis=1, keepdims=True) for row in range(rows)]

    def mix(row, part):
        span = slice(part * size, (part + 1) * size)
        shares = jnp.exp(scores[row, :, span] - tops[row])
        norm[row] = norm[row] + shares if part else shares
        value = lax.dot_general(
            shares.astype(bf16),
            held[row, :latent, span],
            (((1,), (1,)), ((), ())),
            preferred_element_type=f32,
        )
        mixed[row] = mixed[row] + value if part else value

    where_live(mix)
    lines = out.shape[0]
    line = iota((lines, rows * heads), 0)
    a, b, c = line >> 6, (line >> 4) & 3, line & 3
    orders = [sum(PLACE[axis] * v for axis, v in zip(order, (a, b, c))) for order in ORDERS]
    wanted = jnp.where(at[0] == 0, *orders) + heads * ((line >> 2) & 3)
    pick = (wanted == iota((lines, rows * heads), 1)).astype(f32).astype(bf16)
    for row in range(rows):
        value = mixed[row] / jnp.sum(norm[row], axis=1, keepdims=True)
        done[row * heads : (row + 1) * heads, :] = value.astype(bf16)
    out[...] = jnp.dot(pick, done[...], preferred_element_type=f32).astype(bf16)


def attend(lengths, at, queries, cache):
    rows, heads, width = queries.shape
    cache_length = cache.shape[2]
    size = min(CHUNK, cache_length)
    latent = width - 64
    lines = rows * heads
    smem = pl.BlockSpec(memory_space=pltpu.SMEM)
    vmem = pl.BlockSpec(memory_space=pltpu.VMEM)
    return call(
        attend_kernel,
        jax.ShapeDtypeStruct((lines, latent), bf16),
        (lengths, at, queries, cache),
        2 * lines * cache_length * (width + latent),
        56,
        in_specs=[smem, smem, vmem, pl.BlockSpec(memory_space=pltpu.HBM)],
        out_specs=vmem,
        scratch_shapes=[
            pltpu.VMEM(cache.shape, bf16),
            pltpu.VMEM((rows, heads, cache_length), f32),
            pltpu.VMEM((rows, heads, size), f32),
            pltpu.VMEM((rows, heads, size), f32),
            pltpu.VMEM((rows, heads, latent), f32),
            pltpu.VMEM((lines, latent), bf16),
            pltpu.SemaphoreType.DMA((rows, cache_length // size)),
        ],
    )


def heads_kernel(at, latents, w0, w1, w2, w3, out):
    lines = latents.shape[0]
    depth, latent = w0.shape
    line = iota((lines, depth), 0)
    count = lines // SIDE
    gather = (iota((count, lines), 0) == (iota((count, lines), 1) >> 2)).astype(f32).astype(bf16)
    for step, w in enumerate((w0, w1, w2, w3)):
        head = back(at[3], step)
        value = jnp.zeros((lines, depth), f32)
        for k in range(latent // depth):
            span = slice(k * depth, (k + 1) * depth)
            value = value + jnp.dot(latents[:, span], w[:, span], preferred_element_type=f32)
        value = jnp.where((line & 3) == head, value, 0.0).astype(bf16)
        out[head] = jnp.dot(gather, value, preferred_element_type=f32).astype(bf16)


def project_kernel(at, h0, h1, h2, h3, p0, p1, p2, p3, o0, o1, o2, o3, lines):
    packs = (p0, p1, p2, p3)
    heads, _, depth = h0.shape
    block = o0.shape[1] - EXTRA
    latent = p0.shape[1] - block
    a, b, c = at[1], at[2], at[3]
    for step in range(SIDE):
        rows = pl.ds(pl.multiple_of(ahead(a, step) * GROUP, GROUP), GROUP)
        for j, h in enumerate((h0, h1, h2, h3)):
            for k in range(heads):
                lines[step, back(c, j), :, k * depth : (k + 1) * depth] = h[back(c, k), rows, :]
    for step, out in enumerate((o0, o1, o2, o3)):
        left = lines[step].reshape(SIDE * GROUP, heads * depth)
        total = jnp.zeros((SIDE * GROUP, block), f32)
        for k, pack in enumerate(packs):
            total = total + jnp.dot(
                left[:, k * depth : (k + 1) * depth],
                pack[:depth, latent:],
                preferred_element_type=f32,
            )
        out[:, :block] = total.astype(bf16)
        out[:, block:] = jnp.zeros((SIDE * GROUP, EXTRA), bf16)
    move = iota((GROUP, GROUP), 0) == b * 4 + iota((GROUP, GROUP), 1)
    move = (move & (iota((GROUP, GROUP), 1) < 4)).astype(f32).astype(bf16)
    for j, pack in enumerate(packs):
        rows = pl.ds(pl.multiple_of(back(c, j) * GROUP, GROUP), GROUP)
        own = jnp.dot(move, pack[depth:, : block + EXTRA], preferred_element_type=f32)
        o0[rows, :] = (o0[rows, :].astype(f32) + own).astype(bf16)


def norm_kernel(at, s0, s1, s2, s3, gain, out, mine):
    slots = (s0, s1, s2, s3)
    width = gain.shape[1]
    block = width // SIDE
    squares = 0.0
    for slot in slots:
        value = slot[:, :block].astype(f32)
        squares = squares + jnp.sum(value * value, axis=1, keepdims=True)
    factor = lax.rsqrt(squares * (1.0 / width) + epsilon)
    rows = pl.ds(pl.multiple_of(at[3] * GROUP, GROUP), GROUP)
    for step, slot in enumerate(slots):
        to = lanes(back(at[3], step), block)
        out[:, to] = (slot[:, :block].astype(f32) * factor * gain[:, to]).astype(bf16)
        mine[:, to] = slot[rows, :block]
    out[:, width:] = s0[:, block:]


def experts_kernel(count, parts, at, *refs):
    xs, ws, refs = refs[:count], refs[count : 2 * count], refs[2 * count :]
    gates, ups, downs, refs = refs[0:2], refs[2:4], refs[4:6], refs[6:]
    outs, (gate_sum, up_sum, hidden, weights) = refs[:-4], refs[-4:]
    step = pl.program_id(0)
    units = gates[0].shape[2]
    rows = outs[0].shape[0]

    def joined(refs):
        return refs[0][...] if count == 1 else jnp.concatenate([r[...] for r in refs], axis=0)

    @pl.when(step < parts)
    def _():
        x = joined(xs)
        for k in range(2):
            span = slice(k * units, (k + 1) * units)
            gate = jnp.dot(x, gates[k][0], preferred_element_type=f32)
            up = jnp.dot(x, ups[k][0], preferred_element_type=f32)

            @pl.when(step == 0)
            def _():
                gate_sum[:, span] = gate
                up_sum[:, span] = up

            @pl.when(step > 0)
            def _():
                gate_sum[:, span] += gate
                up_sum[:, span] += up

    @pl.when(step == parts - 1)
    def _():
        gate = gate_sum[...]
        hidden[...] = (gate * (1.0 / (1.0 + jnp.exp(-gate))) * up_sum[...]).astype(bf16)
        told = joined(ws).astype(f32)
        for k in range(2):
            chosen = iota(told.shape, 1) == at[4 + k]
            weight = jnp.sum(jnp.where(chosen, told, 0.0), axis=1, keepdims=True)
            weights[k] = jnp.broadcast_to(weight, told.shape)

    @pl.when(step >= parts)
    def _():
        total = 0.0
        for k in range(2):
            value = jnp.dot(
                hidden[:, k * units : (k + 1) * units], downs[k][0], preferred_element_type=f32
            )
            total = total + value * weights[k][:, 0:1]
        for k, out in enumerate(outs):
            out[...] = total[k * rows : (k + 1) * rows].astype(bf16)


def experts(at, slots, gates, ups, downs, pieces):
    count, parts = len(slots), 2
    rows = slots[0].shape[0]
    width, units = gates[0].shape[1:]
    block = width // parts

    def first(i):
        return jnp.minimum(i, parts - 1)

    def second(i):
        return jnp.maximum(i - parts, 0)

    in_specs = [pl.BlockSpec(memory_space=pltpu.SMEM)]
    in_specs += [pl.BlockSpec((rows, block), lambda i: (0, first(i)))] * count
    in_specs += [pl.BlockSpec((rows, EXTRA), lambda i: (0, width // EXTRA))] * count
    in_specs += [pl.BlockSpec((1, block, units), lambda i: (0, first(i), 0))] * 4
    in_specs += [pl.BlockSpec((1, units, block), lambda i: (0, 0, second(i)))] * 2
    return call(
        functools.partial(experts_kernel, count, parts),
        [jax.ShapeDtypeStruct((count * rows // pieces, width), bf16)] * pieces,
        (at, *slots, *slots, *gates, *ups, *downs),
        12 * count * rows * width * units,
        28,
        grid=(2 * parts,),
        in_specs=in_specs,
        out_specs=[pl.BlockSpec((count * rows // pieces, block), lambda i: (0, second(i)))]
        * pieces,
        scratch_shapes=[
            pltpu.VMEM((count * rows, 2 * units), f32),
            pltpu.VMEM((count * rows, 2 * units), f32),
            pltpu.VMEM((count * rows, 2 * units), bf16),
            pltpu.VMEM((2, count * rows, EXTRA), f32),
        ],
    )


def load_kernel(at, x, *refs):
    sources, out, held, refs = refs[:6], refs[6], refs[7:13], refs[13:]
    gate_sum, up_sum, hidden, sems = refs
    gates, ups, downs = held[0:2], held[2:4], held[4:6]
    _, width, units = gates[0].shape
    step = width // SIDE

    def copy(k, i):
        span = pl.ds(i * step, step)
        where = (0, span) if k < 4 else (0, slice(None), span)
        return pltpu.make_async_copy(sources[k].at[where], held[k].at[where], sems.at[k, i])

    for i in range(SIDE):
        for k in range(4):
            copy(k, i).start()
    for i in range(SIDE):
        for k in (4, 5):
            copy(k, i).start()
    for i in range(SIDE):
        span = slice(i * step, (i + 1) * step)
        for k in range(4):
            copy(k, i).wait()
        for k in range(2):
            to = slice(k * units, (k + 1) * units)
            gate = jnp.dot(x[:, span], gates[k][0, span, :], preferred_element_type=f32)
            up = jnp.dot(x[:, span], ups[k][0, span, :], preferred_element_type=f32)
            gate_sum[:, to] = gate_sum[:, to] + gate if i else gate
            up_sum[:, to] = up_sum[:, to] + up if i else up
    gate = gate_sum[...]
    hidden[...] = (gate * (1.0 / (1.0 + jnp.exp(-gate))) * up_sum[...]).astype(bf16)
    told = x[:, width:].astype(f32)
    weights = []
    for k in range(2):
        chosen = iota(told.shape, 1) == at[4 + k]
        weights.append(jnp.sum(jnp.where(chosen, told, 0.0), axis=1, keepdims=True))
    for i in range(SIDE):
        span = slice(i * step, (i + 1) * step)
        total = 0.0
        for k in range(2):
            copy(4 + k, i).wait()
            left = hidden[:, k * units : (k + 1) * units]
            value = jnp.dot(left, downs[k][0, :, span], preferred_element_type=f32)
            total = total + value * weights[k]
        out[:, span] = total.astype(bf16)


def experts_and_load(at, x, gates, ups, downs):
    rows = x.shape[0]
    width, units = gates[0].shape[1:]
    blocks = (*gates, *ups, *downs)
    smem, vmem = [pl.BlockSpec(memory_space=m) for m in (pltpu.SMEM, pltpu.VMEM)]
    out, *held = call(
        load_kernel,
        [jax.ShapeDtypeStruct((rows, width), bf16)]
        + [jax.ShapeDtypeStruct(v.shape, bf16) for v in blocks],
        (at, x, *blocks),
        12 * rows * width * units,
        30,
        in_specs=[smem, vmem] + [pl.BlockSpec(memory_space=pltpu.HBM)] * 6,
        out_specs=[vmem] * 7,
        scratch_shapes=[
            pltpu.VMEM((rows, 2 * units), f32),
            pltpu.VMEM((rows, 2 * units), f32),
            pltpu.VMEM((rows, 2 * units), bf16),
            pltpu.SemaphoreType.DMA((6, SIDE)),
        ],
    )
    return out, held[0:2], held[2:4], held[4:6]


def sum_kernel(at, p0, p1, p2, p3, out):
    rows = out.shape[1]
    for i in range(p0.shape[0] // GROUP):
        span = slice(i * GROUP, (i + 1) * GROUP)
        total = sum(p[span, :].astype(f32) for p in (p0, p1, p2, p3))
        for j in range(GROUP // rows):
            out[i * (GROUP // rows) + j] = total[j * rows : (j + 1) * rows].astype(bf16)


def on_device(
    queries,
    latent_cache,
    lengths,
    residual,
    w_uv,
    w_out,
    norm_gain,
    expert_ids,
    gate_values,
    w_gate,
    w_up,
    w_down,
):
    role, dev = lax.axis_index("role"), lax.axis_index("dev")
    a, b, c = [
        jnp.where(role == 0, *[dev // PLACE[order[i]] % SIDE for order in ORDERS]) for i in range(3)
    ]
    per_expert = 128 // EXPERTS
    experts_here = [(role * 64 + dev) // per_expert, ((1 - role) * 64 + dev) // per_expert]
    at = jnp.stack([role, a, b, c, *experts_here, role, role]).astype(jnp.int32)
    rows, width = residual.shape
    latent, depth = w_uv.shape[1:]
    block = width // SIDE
    count = GROUP * SIDE

    shape = jax.ShapeDtypeStruct((depth + GROUP, latent + block), bf16)
    packs = call(
        bundle_kernel,
        [shape] * SIDE,
        (at, w_out, w_uv, residual, expert_ids, gate_values),
        0,
        60,
        grid=(1,),
        in_specs=[pl.BlockSpec(memory_space=pltpu.SMEM)]
        + [
            pl.BlockSpec(v.shape, lambda i, n=v.ndim: (0,) * n)
            for v in (w_out, w_uv, residual, expert_ids, gate_values)
        ],
        out_specs=[pl.BlockSpec(shape.shape, lambda i: (0, 0))] * SIDE,
    )
    packs = [packs[0]] + [shift(packs[s], "c", s) for s in (1, 2, 3)]
    gates, ups, downs = [(w, swap_cores(w)) for w in (w_gate, w_up, w_down)]

    sent = attend(lengths, at, queries, latent_cache.swapaxes(1, 2)).reshape(16, SIDE * rows, latent)
    got = lax.all_to_all(sent, AXES, 0, 0, axis_index_groups=groups("ab"), tiled=True)
    got, gates, ups, downs = lax.optimization_barrier((got, gates, ups, downs))
    got = got.reshape(-1, latent)
    vmem = pl.BlockSpec(memory_space=pltpu.VMEM)
    head_out = call(
        heads_kernel,
        jax.ShapeDtypeStruct((SIDE, count, depth), bf16),
        (at, got, *packs),
        2 * SIDE * got.size * depth,
        16,
        grid=(1,),
        in_specs=[pl.BlockSpec(memory_space=pltpu.SMEM), vmem]
        + [pl.BlockSpec((depth, latent), lambda i: (0, 0))] * SIDE,
        out_specs=vmem,
    )
    gathered = shifts(head_out, "c")
    partial = call(
        project_kernel,
        [jax.ShapeDtypeStruct((count, block + EXTRA), bf16)] * SIDE,
        (at, *gathered, *packs),
        2 * SIDE * count * SIDE * depth * block,
        24,
        scratch_shapes=[pltpu.VMEM((SIDE, SIDE, GROUP, SIDE * depth), bf16)],
    )

    def added(parts):
        return functools.reduce(lambda u, v: u + v, [p.astype(f32) for p in parts]).astype(bf16)

    total = added([partial[0]] + [shift(partial[s], "a", s) for s in (2, 1, 3)])
    attended = added(shifts(total, "b"))
    columns = shifts(attended, "c")
    normed, mine = call(
        norm_kernel,
        [
            jax.ShapeDtypeStruct((count, width + EXTRA), bf16),
            jax.ShapeDtypeStruct((GROUP, width), bf16),
        ],
        (at, *columns, norm_gain.astype(f32).reshape(1, width)),
        0,
        16,
    )

    own_sum, gates, ups, downs = experts_and_load(at, normed, gates, ups, downs)
    near = [shift(normed, "a", s) for s in (1, 3)]
    near, own_sum = lax.optimization_barrier((near, own_sum))
    half = count // 2
    far = [shift(near[0][:half], "a", 1), shift(near[1][half:], "a", 3)]
    near_sums = experts(at, near, gates, ups, downs, 2)
    (far_sum,) = experts(at, far, gates, ups, downs, 1)
    sums = [shift(near_sums[0], "a", -1), shift(near_sums[1], "a", -3), shift(far_sum, "a", -2)]
    last = call(
        sum_kernel, jax.ShapeDtypeStruct((16, rows, width), bf16), (at, own_sum, *sums), 0, 16
    )
    last = lax.all_to_all(last, AXES, 0, 0, axis_index_groups=groups("cb"), tiled=True)
    combined = jnp.sum(last.astype(f32), axis=0)
    mine = lax.dynamic_slice_in_dim(mine, b * rows, rows, 0)
    return (mine.astype(f32) + combined).astype(bf16)


def solution(mesh):
    return jax.shard_map(
        on_device,
        mesh=mesh,
        in_specs=(
            P(("role", "dev"), None, None),
            P(("role", "dev"), None, None),
            P(("role", "dev")),
            P(("role", "dev"), None),
            P("dev", None, None),
            P("dev", None),
            P(),
            P(("role", "dev"), None),
            P(("role", "dev"), None),
            P(("role", "dev"), None, None),
            P(("role", "dev"), None, None),
            P(("role", "dev"), None, None),
        ),
        out_specs=P(("role", "dev"), None),
        check_vma=False,
    )
```
